256 devices in a mesh: role: 8 (over x, core), seq: 8 (over z_lo, y), prompt: 4 (over z_hi).
Axes of the slice: x: 4, y: 4, z: 8 (z_hi: 4, z_lo: 2; z = z_hi * 2 + z_lo), core: 2. Of those that a mesh axis runs over, the one named last changes fastest.
Arguments:
- queries: bfloat16 [32768, 4096], P(('prompt', 'role', 'seq')), parts along dimension 0, may hold values from -8 to 8
- keys: bfloat16 [32768, 2048], P(('prompt', 'role', 'seq')), parts along dimension 0, may hold values from -8 to 8
- values: bfloat16 [32768, 2048], P(('prompt', 'role', 'seq')), parts along dimension 0, may hold values from -6 to 6
- answer_query_rows: bfloat16 [512, 4, 4096], P(('prompt', 'role'), None, 'seq'), parts along dimension 0, may hold values from -8 to 8
- answer_key_rows: bfloat16 [512, 4, 2048], P(('prompt', 'role'), None, 'seq'), parts along dimension 0, may hold values from -8 to 8
- answer_value_rows: bfloat16 [512, 4, 2048], P(('prompt', 'role'), None, 'seq'), parts along dimension 0, may hold values from -6 to 6
Outputs:
- prefill_out: bfloat16 [32768, 4096], P(('prompt', 'role', 'seq')), parts along dimension 0
- answer_out: bfloat16 [512, 4, 4096], P(('prompt', 'role'), None, 'seq'), parts along dimension 0
The draws below stay inside these ranges and needn't reach their ends.
There are 4 independent parts, one for each index of `prompt`. The reference program is written for one: setup_inputs(seed, part) draws one part's arguments, and reference() takes and returns one part's arrays. A program takes and returns all parts, laid end to end along the dimension named above; each array names one. Nothing has to cross between parts.
All inputs are finite; a program needn't handle non-finite values.
Results may differ from the reference program's by a relative error of at most 0.015.
Values may be sent and summed in bfloat16 or wider, within the bound.
No kernel may reach another device: no remote copies, remote signals or barrier semaphores. Data moves between devices by JAX's collectives and lax.ppermute only.
A program may use at most 64 MiB of HBM per device.

```python
import jax
import jax.numpy as jnp
from jax import lax

QUERY_HEADS = 32
KEY_VALUE_HEADS = 16
HEAD_SIZE = 128
ROWS_DEV = 128
ANSWER_STEPS = 4
PROMPT_LENGTH = 8192
ANSWER_TOTAL = 128
N_ROLE = 8
N_SEQ = 8


def coarse_score_grid(key, array_shape, base):
    random_jitter = jax.random.normal(key, array_shape, jnp.float32)
    return jnp.clip(base * random_jitter, -8.0, 8.0)


def answer_field(key, base):
    return coarse_score_grid(jax.random.fold_in(key, 500), (ANSWER_TOTAL, ANSWER_STEPS, QUERY_HEADS * HEAD_SIZE), base)


def draw_queries(key, part):
    key = jax.random.fold_in(key, 1)
    score_grid = coarse_score_grid(key, (PROMPT_LENGTH, QUERY_HEADS * HEAD_SIZE), 2.5)
    return score_grid.astype(jnp.bfloat16)


def draw_keys(key, part):
    key = jax.random.fold_in(key, 2)
    score_grid = coarse_score_grid(key, (PROMPT_LENGTH, KEY_VALUE_HEADS * HEAD_SIZE), 1.0)
    return score_grid.astype(jnp.bfloat16)


def draw_answer_query_rows(key, part):
    score_grid = answer_field(key, 2.5)
    return score_grid.astype(jnp.bfloat16)


def draw_answer_key_rows(key, part):
    common_prompt = answer_field(key, 2.5)
    key = jax.random.fold_in(key, 4)
    leading_heads = common_prompt.reshape(ANSWER_TOTAL, ANSWER_STEPS, KEY_VALUE_HEADS, QUERY_HEADS // KEY_VALUE_HEADS, HEAD_SIZE)[:, :, :, 0, :].reshape(ANSWER_TOTAL, ANSWER_STEPS, KEY_VALUE_HEADS * HEAD_SIZE)
    random_jitter = jax.random.normal(key, (ANSWER_TOTAL, ANSWER_STEPS, KEY_VALUE_HEADS * HEAD_SIZE), jnp.float32)
    return jnp.clip(0.18 * leading_heads + random_jitter, -8.0, 8.0).astype(jnp.bfloat16)


def levels(stream_key, shape, cuts, least, high):
    def one(axis_at, blocks):
        draws = jax.random.uniform(jax.random.fold_in(jax.random.fold_in(stream_key, 6), axis_at), (blocks,), jnp.float32, least / len(cuts), high / len(cuts))
        return jnp.repeat(jnp.exp(draws), shape[axis_at] // blocks).reshape((-1,) + (1,) * (len(shape) - axis_at - 1))

    loudness = one(*cuts[0])
    for cut in cuts[1:]:
        loudness = loudness * one(*cut)
    return loudness


def normal_values(key, extent, deviation, reach, shards=(), held_as=jnp.bfloat16):
    factor_of = levels(key, extent, shards, -0.22, 0.18) if shards else 1.0
    result = jax.random.normal(key, extent, jnp.float32) * deviation * factor_of
    return jnp.minimum(jnp.maximum(result, -reach), reach).astype(held_as)


def setup_inputs(seed: int = 0, part: int = 0) -> dict:
    seeds = jax.random.split(jax.random.key(seed), 7)
    own_keys = jax.random.split(jax.random.fold_in(seeds[6], part), 7)
    return {
        "queries": draw_queries(jax.random.fold_in(jax.random.fold_in(seeds[6], part), 71), part),
        "keys": draw_keys(jax.random.fold_in(jax.random.fold_in(seeds[6], part), 71), part),
        "values": normal_values(own_keys[2], (PROMPT_LENGTH, KEY_VALUE_HEADS * HEAD_SIZE), 1.0, 6.0, ((0, 64),)),
        "answer_query_rows": draw_answer_query_rows(jax.random.fold_in(jax.random.fold_in(seeds[6], part), 71), part),
        "answer_key_rows": draw_answer_key_rows(jax.random.fold_in(jax.random.fold_in(seeds[6], part), 71), part),
        "answer_value_rows": normal_values(own_keys[5], (ANSWER_TOTAL, ANSWER_STEPS, KEY_VALUE_HEADS * HEAD_SIZE), 1.0, 6.0, ((0, 8), (2, 8))),
    }


def rounded(weights):
    return lax.optimization_barrier(weights.astype(jnp.bfloat16)).astype(jnp.float32)


def reference(queries, keys, values, answer_query_rows, answer_key_rows, answer_value_rows):
    group_width = QUERY_HEADS // KEY_VALUE_HEADS
    score_scale = 168.0 ** -0.5
    block = ROWS_DEV * N_SEQ
    query_head_rows = queries.reshape(PROMPT_LENGTH, KEY_VALUE_HEADS, group_width, HEAD_SIZE)
    key_head_rows = keys.reshape(PROMPT_LENGTH, KEY_VALUE_HEADS, HEAD_SIZE)
    value_head_rows = values.reshape(PROMPT_LENGTH, KEY_VALUE_HEADS, HEAD_SIZE)
    key_places = jnp.arange(PROMPT_LENGTH, dtype=jnp.int32)

    def prompt_head_output(head_index):
        head_q = lax.dynamic_index_in_dim(query_head_rows, head_index, 1, False).astype(jnp.float32)
        head_k = lax.dynamic_index_in_dim(key_head_rows, head_index, 1, False).astype(jnp.float32)
        head_v = lax.dynamic_index_in_dim(value_head_rows, head_index, 1, False).astype(jnp.float32)

        def prompt_block(block_index):
            start = (block_index * block).astype(jnp.int32)
            block_q = lax.dynamic_slice_in_dim(head_q, start, block, 0)
            scores = jnp.einsum("igd,jd->igj", block_q, head_k) * score_scale
            places = start + jnp.arange(block, dtype=jnp.int32)
            allowed = key_places[None, None, :] <= places[:, None, None]
            masked = jnp.where(allowed, scores, -jnp.inf)
            highest = jnp.max(masked, axis=-1, keepdims=True)
            expos = jnp.where(allowed, jnp.exp(masked - highest), 0.0)
            totals = jnp.sum(expos, axis=-1, keepdims=True)
            return jnp.einsum("igj,jd->igd", rounded(expos), head_v) / totals

        blocks = lax.map(prompt_block, jnp.arange(N_ROLE, dtype=jnp.int32))
        return blocks.reshape(PROMPT_LENGTH, group_width, HEAD_SIZE)

    prompt_output_all = lax.map(prompt_head_output, jnp.arange(KEY_VALUE_HEADS, dtype=jnp.int32))
    prefill_out = jnp.transpose(prompt_output_all, (1, 0, 2, 3)).reshape(PROMPT_LENGTH, QUERY_HEADS * HEAD_SIZE).astype(jnp.bfloat16)

    answer_head_outputs = answer_query_rows.reshape(ANSWER_TOTAL, ANSWER_STEPS, KEY_VALUE_HEADS, group_width, HEAD_SIZE)
    answer_self_keys = answer_key_rows.reshape(ANSWER_TOTAL, ANSWER_STEPS, KEY_VALUE_HEADS, HEAD_SIZE)
    answer_self_values = answer_value_rows.reshape(ANSWER_TOTAL, ANSWER_STEPS, KEY_VALUE_HEADS, HEAD_SIZE)
    step_order = jnp.arange(ANSWER_STEPS, dtype=jnp.int32)
    own_allowed = (step_order[None, :] <= step_order[:, None])[None, :, None, :]

    def answer_head_output(head_index):
        head_q = lax.dynamic_index_in_dim(answer_head_outputs, head_index, 2, False).astype(jnp.float32)
        head_k = lax.dynamic_index_in_dim(key_head_rows, head_index, 1, False).astype(jnp.float32)
        head_v = lax.dynamic_index_in_dim(value_head_rows, head_index, 1, False).astype(jnp.float32)
        near_k = lax.dynamic_index_in_dim(answer_self_keys, head_index, 2, False).astype(jnp.float32)
        near_v = lax.dynamic_index_in_dim(answer_self_values, head_index, 2, False).astype(jnp.float32)
        far_scores = jnp.einsum("atgd,jd->atgj", head_q, head_k) * score_scale
        near_scores = jnp.einsum("atgd,aud->atgu", head_q, near_k) * score_scale
        near_scores = jnp.where(own_allowed, near_scores, -jnp.inf)
        highest = jnp.maximum(jnp.max(far_scores, axis=-1, keepdims=True), jnp.max(near_scores, axis=-1, keepdims=True))
        far_expos = jnp.exp(far_scores - highest)
        near_expos = jnp.where(own_allowed, jnp.exp(near_scores - highest), 0.0)
        totals = jnp.sum(far_expos, axis=-1, keepdims=True) + jnp.sum(near_expos, axis=-1, keepdims=True)
        summed = jnp.einsum("atgj,jd->atgd", rounded(far_expos), head_v) + jnp.einsum("atgu,aud->atgd", rounded(near_expos), near_v)
        return summed / totals

    answer_output_all = lax.map(answer_head_output, jnp.arange(KEY_VALUE_HEADS, dtype=jnp.int32))
    answer_out = jnp.transpose(answer_output_all, (1, 2, 0, 3, 4)).reshape(ANSWER_TOTAL, ANSWER_STEPS, QUERY_HEADS * HEAD_SIZE).astype(jnp.bfloat16)
    return prefill_out, answer_out
```

```python
import functools
import math

import jax
import jax.numpy as jnp
from jax import lax
from jax.experimental import pallas as pl
from jax.experimental.pallas import tpu as pltpu
from jax.sharding import PartitionSpec as P


HEAD = 128
HALF = 64
score_scale = 168.0 ** (-0.5)
scale2 = score_scale * math.log2(math.e)
masked = -1e30
safe_square = (100.0 / scale2) ** 2
VMEM_LIMIT = 60 * 1024 * 1024
bf16, f32 = jnp.bfloat16, jnp.float32
rows_rows = (((1,), (1,)), ((), ()))


def pack_kernel(q_ref, k_ref, v_ref, out_ref):
    for kv in range(2):
        for seq in range(8):
            g = 2 * seq + kv
            k = k_ref[:, g * HEAD : (g + 1) * HEAD]
            vt = v_ref[:, g * HEAD : (g + 1) * HEAD].T
            for half in range(2):
                for core in range(2):
                    dest = ((2 * kv + half) * 2 + core) * 8 + seq
                    h = 2 * g + core
                    out_ref[dest, 0:HALF, :] = q_ref[
                        half * HALF : (half + 1) * HALF, h * HEAD : (h + 1) * HEAD
                    ]
                    out_ref[dest, HALF:, :] = k if core == 0 else vt


def unpack_kernel(in_ref, out_ref):
    for kv in range(2):
        for half in range(2):
            for core in range(2):
                for seq in range(8):
                    src = ((2 * kv + half) * 2 + core) * 8 + seq
                    h = 4 * seq + 2 * kv + core
                    out_ref[half * HALF : (half + 1) * HALF, h * HEAD : (h + 1) * HEAD] = in_ref[src]


def bring(own_ref, other_ref, ks, vt, sems):
    core = lax.axis_index("role") % 2

    def both(first, second):
        a = pltpu.make_async_copy(first, ks, sems.at[0])
        b = pltpu.make_async_copy(second, vt, sems.at[1])
        a.start()
        b.start()
        a.wait()
        b.wait()

    @pl.when(core == 0)
    def _():
        both(own_ref, other_ref)

    @pl.when(core == 1)
    def _():
        both(other_ref, own_ref)


def largest_square(rows):
    squares = lax.dot_general(
        jnp.ones((16, HEAD), bf16), rows * rows, rows_rows, preferred_element_type=f32
    )
    return jnp.max(squares)


def add_keys(q, keys, values_t, allowed, first, acc, tot, top, shifted):
    s = lax.dot_general(keys, q, rows_rows, preferred_element_type=f32)
    if allowed is not None:
        s = jnp.where(allowed, s, masked)
    n, w = s.shape
    s = s * scale2
    if shifted:
        old = top[:, first:]
        new = jnp.maximum(old, jnp.max(s, axis=0, keepdims=True))
        shrink = jnp.exp2(old - new)
        s = s - new
        top[:, first:] = new
        tot[:, first:] = tot[:, first:] * shrink
        acc[:, first:] = acc[:, first:] * shrink
    p = jnp.exp2(s)
    tot[:, first:] += jnp.sum(p.reshape(n // 8, 8, w), axis=0)
    acc[:, first:] += jnp.dot(values_t, p.astype(bf16), preferred_element_type=f32)


def key_block(ks, vt, n, count):
    keys = ks[pl.ds(n, count)].reshape(count * HEAD, HEAD)
    values_t = jnp.concatenate([vt[n + i] for i in range(count)], axis=1)
    return keys, values_t


def clear(acc, tot, top):
    acc[...] = jnp.zeros_like(acc)
    tot[...] = jnp.zeros_like(tot)
    top[...] = jnp.full_like(top, masked)


def finish(acc, tot):
    total = jnp.sum(tot[...], axis=0, keepdims=True)
    return (acc[...] / total).T.astype(bf16)


BLOCK_N = 16
KEY_N = 8
DIAG_N = 4


def prompt_kernel(q_ref, own_ref, other_ref, o_ref, ks, vt, acc, tot, top, k_square, sems):
    i = pl.program_id(0)
    half = (lax.axis_index("role") // 2) % 2

    @pl.when(i == 0)
    def _():
        bring(own_ref, other_ref, ks, vt, sems)
        k_square[0] = largest_square(ks[...].reshape(-1, HEAD))

    q = q_ref[...].reshape(BLOCK_N * HALF, HEAD)
    safe = largest_square(q) * k_square[0] <= safe_square
    clear(acc, tot, top)

    def run(shifted):
        def body(t, carry):
            keys, values_t = key_block(ks, vt, t * KEY_N, KEY_N)
            add_keys(q, keys, values_t, None, 0, acc, tot, top, shifted)
            return carry

        lax.fori_loop(0, i * (BLOCK_N // KEY_N), body, 0)
        for c in range(BLOCK_N // DIAG_N):
            first = c * DIAG_N * HALF
            keys, values_t = key_block(ks, vt, i * BLOCK_N + c * DIAG_N, DIAG_N)
            shape = (DIAG_N * HEAD, BLOCK_N * HALF - first)
            key_place = lax.broadcasted_iota(jnp.int32, shape, 0)
            row = lax.broadcasted_iota(jnp.int32, shape, 1)
            row_place = (row // HALF) * HEAD + row % HALF + half * HALF
            add_keys(
                q[first:], keys, values_t, key_place <= row_place, first, acc, tot, top, shifted
            )

    @pl.when(safe)
    def _():
        run(False)

    @pl.when(jnp.logical_not(safe))
    def _():
        run(True)

    o_ref[...] = finish(acc, tot).reshape(BLOCK_N, HALF, HEAD)


def answer_kernel(
    q_ref, k_ref, v_ref, own_ref, other_ref, o_ref, ks, vt, acc, tot, top, sems
):
    bring(own_ref, other_ref, ks, vt, sems)
    q = q_ref[...]
    near = k_ref[...]
    k_square = jnp.maximum(largest_square(ks[...].reshape(-1, HEAD)), largest_square(near))
    safe = largest_square(q) * k_square <= safe_square
    clear(acc, tot, top)
    count = q.shape[0]

    def run(shifted):
        def body(t, carry):
            keys, values_t = key_block(ks, vt, t * KEY_N, KEY_N)
            add_keys(q, keys, values_t, None, 0, acc, tot, top, shifted)
            return carry

        lax.fori_loop(0, ks.shape[0] // KEY_N, body, 0)
        u = lax.broadcasted_iota(jnp.int32, (count, count), 0)
        t = lax.broadcasted_iota(jnp.int32, (count, count), 1)
        allowed = (u // 4 == t // 4) & (u <= t)
        add_keys(q, near, v_ref[...].T, allowed, 0, acc, tot, top, shifted)

    @pl.when(safe)
    def _():
        run(False)

    @pl.when(jnp.logical_not(safe))
    def _():
        run(True)

    o_ref[...] = finish(acc, tot)


def on_device(queries, keys, values, answer_query_rows, answer_key_rows, answer_value_rows):
    params = pltpu.CompilerParams(vmem_limit_bytes=VMEM_LIMIT)
    both_axes = ("role", "seq")
    swap_cores = [(r, r ^ 1) for r in range(8)]
    swap_chips = [(r, 2 * (3 - r // 2) + r % 2) for r in range(8)]
    role = lax.axis_index("role")
    core_0 = role % 2 == 0
    low = role // 4 == 0
    whole = pl.BlockSpec(memory_space=pltpu.VMEM)
    anywhere = pl.BlockSpec(memory_space=pl.ANY)

    packed = pl.pallas_call(
        pack_kernel,
        out_shape=jax.ShapeDtypeStruct((64, HALF + HEAD, HEAD), bf16),
        in_specs=[whole] * 3,
        out_specs=whole,
        compiler_params=params,
    )(queries, keys, values)
    arrived = lax.all_to_all(packed, both_axes, split_axis=0, concat_axis=0, tiled=True)
    own = arrived[:, HALF:, :]
    other = lax.ppermute(own, "role", swap_cores)

    answers, steps = answer_query_rows.shape[:2]
    rows = answers * steps
    mixed = jnp.concatenate(
        [
            answer_query_rows.reshape(rows, 2, 2 * HEAD),
            answer_key_rows.reshape(rows, 2, HEAD),
            answer_value_rows.reshape(rows, 2, HEAD),
        ],
        axis=-1,
    )
    kept = jnp.where(low, mixed[:, 0], mixed[:, 1])
    sent = jnp.where(low, mixed[:, 1], mixed[:, 0])
    two = jnp.stack([kept, lax.ppermute(sent, "role", swap_chips)])
    q_kept = jnp.where(core_0, two[..., :HEAD], two[..., HEAD : 2 * HEAD])
    q_sent = jnp.where(core_0, two[..., HEAD : 2 * HEAD], two[..., :HEAD])
    near = two[..., 2 * HEAD :]
    got = lax.ppermute(jnp.concatenate([q_sent, near], axis=-1), "role", swap_cores)
    answer_q = jnp.concatenate([q_kept, got[..., :HEAD]]).reshape(4 * rows, HEAD)
    near = jnp.concatenate([near, got[..., HEAD:]]).reshape(4 * rows, 2 * HEAD)

    blocks = 64
    width = BLOCK_N * HALF
    attended = pl.pallas_call(
        prompt_kernel,
        out_shape=jax.ShapeDtypeStruct((blocks, HALF, HEAD), bf16),
        grid=(blocks // BLOCK_N,),
        in_specs=[pl.BlockSpec((BLOCK_N, HALF, HEAD), lambda i: (i, 0, 0)), anywhere, anywhere],
        out_specs=pl.BlockSpec((BLOCK_N, HALF, HEAD), lambda i: (i, 0, 0)),
        scratch_shapes=[
            pltpu.VMEM((blocks, HEAD, HEAD), bf16),
            pltpu.VMEM((blocks, HEAD, HEAD), bf16),
            pltpu.VMEM((HEAD, width), f32),
            pltpu.VMEM((8, width), f32),
            pltpu.VMEM((1, width), f32),
            pltpu.SMEM((1,), f32),
            pltpu.SemaphoreType.DMA((2,)),
        ],
        compiler_params=params,
    )(arrived, own, other)
    returned = lax.all_to_all(attended, both_axes, split_axis=0, concat_axis=0, tiled=True)

    answered = pl.pallas_call(
        answer_kernel,
        out_shape=jax.ShapeDtypeStruct((4 * rows, HEAD), bf16),
        in_specs=[whole] * 3 + [anywhere] * 2,
        out_specs=whole,
        scratch_shapes=[
            pltpu.VMEM((blocks, HEAD, HEAD), bf16),
            pltpu.VMEM((blocks, HEAD, HEAD), bf16),
            pltpu.VMEM((HEAD, 4 * rows), f32),
            pltpu.VMEM((8, 4 * rows), f32),
            pltpu.VMEM((1, 4 * rows), f32),
            pltpu.SemaphoreType.DMA((2,)),
        ],
        compiler_params=params,
        cost_estimate=pl.CostEstimate(
            flops=4 * 4 * rows * 8192 * HEAD, bytes_accessed=1 << 22, transcendentals=4 * rows * 8192
        ),
    )(answer_q, near[:, :HEAD], near[:, HEAD:], own, other)
    answered = answered.reshape(2, 2, rows, HEAD)
    back = lax.ppermute(answered[1], "role", swap_cores)
    pair = jnp.concatenate(
        [jnp.where(core_0, answered[0], back), jnp.where(core_0, back, answered[0])], axis=-1
    )
    home = lax.ppermute(pair[1], "role", swap_chips)
    answer_out = jnp.concatenate(
        [jnp.where(low, pair[0], home), jnp.where(low, home, pair[0])], axis=-1
    ).reshape(answers, steps, 4 * HEAD)

    prefill_out = pl.pallas_call(
        unpack_kernel,
        out_shape=jax.ShapeDtypeStruct((HEAD, 32 * HEAD), bf16),
        in_specs=[whole],
        out_specs=whole,
        compiler_params=params,
    )(returned)
    return prefill_out, answer_out


def solution(mesh):
    return jax.shard_map(
        on_device,
        mesh=mesh,
        in_specs=(
            P(("prompt", "role", "seq"), None),
            P(("prompt", "role", "seq"), None),
            P(("prompt", "role", "seq"), None),
            P(("prompt", "role"), None, "seq"),
            P(("prompt", "role"), None, "seq"),
            P(("prompt", "role"), None, "seq"),
        ),
        out_specs=(P(("prompt", "role", "seq"), None), P(("prompt", "role"), None, "seq")),
        check_vma=False,
    )
```

```python
import math

import jax
import jax.numpy as jnp
from jax import lax
from jax.experimental import pallas as pl
from jax.experimental.pallas import tpu as pltpu
from jax.sharding import Mesh, PartitionSpec as P


HEAD = 128
score_scale = 168.0 ** (-0.5)
scale2 = score_scale * math.log2(math.e)
masked = -1e30
safe_square = (100.0 / scale2) ** 2
VMEM_LIMIT = 62 * 1024 * 1024
bf16, f32 = jnp.bfloat16, jnp.float32
rows_rows = (((1,), (1,)), ((), ()))

UNITS = 32
SOME = 4
PART = 8
WIDTH = PART * HEAD
PARTS = UNITS // PART


def key_head(x, y):
    return 2 * (4 * (x // 2) + y) + x % 2


def dest(x, core, y):
    return (2 * x + core) * 4 + y


def heads():
    return [(x, core, y) for x in range(4) for core in range(2) for y in range(4)]


def half_heads():
    return [
        ((2 * p + core) * 4 + y, 2 * y + p, core)
        for p in range(2)
        for core in range(2)
        for y in range(4)
    ]


def pack_keys_kernel(k_ref, v_ref, out_ref):
    for to, g, core in half_heads():
        at = g * HEAD
        if core == 0:
            out_ref[to] = k_ref[:, at : at + HEAD]
        else:
            out_ref[to] = v_ref[:, at : at + HEAD].T


def pack_queries_kernel(q_ref, aq_ref, ak_ref, av_ref, out_ref, kept_ref, sent_ref):
    for x, core, y in heads():
        at = (2 * key_head(x, y) + core) * HEAD
        out_ref[dest(x, core, y)] = q_ref[:, at : at + HEAD]
    odd = lax.axis_index("x") % 2
    here = lax.axis_index("core")
    rows = kept_ref.shape[1]
    q_rows = aq_ref[...].reshape(rows, 4 * HEAD)
    k_rows = ak_ref[...].reshape(rows, 2 * HEAD)
    v_rows = av_ref[...].reshape(rows, 2 * HEAD)
    for p in range(2):
        at = (odd + p) % 2
        near = [rows_of[:, p * HEAD : (p + 1) * HEAD] for rows_of in (k_rows, v_rows)]
        both = [q_rows[:, (2 * p + core) * HEAD : (2 * p + core + 1) * HEAD] for core in range(2)]
        for to_ref, mine in ((kept_ref, here == 0), (sent_ref, here == 1)):
            to_ref[at] = jnp.concatenate([jnp.where(mine, both[0], both[1]), *near], axis=1)


def unpack_kernel(in_ref, out_ref):
    for place, g, core in half_heads():
        at = (2 * g + core) * HEAD
        out_ref[:, at : at + HEAD] = in_ref[place]


def copies(core, own_ref, got_ref, ks, vt, sems, part):
    at = pl.ds(part * PART, PART)
    key_ref, value_ref = (own_ref, got_ref) if core == 0 else (got_ref, own_ref)
    return (
        pltpu.make_async_copy(key_ref.at[at], ks.at[at], sems.at[0, part]),
        pltpu.make_async_copy(value_ref.at[at], vt.at[at], sems.at[1, part]),
    )


def start_keys(part, *refs):
    here = lax.axis_index("core")
    for core in range(2):

        @pl.when(here == core)
        def _():
            for copy in copies(core, *refs, part):
                copy.start()


def wait_keys(part, *refs):
    for copy in copies(0, *refs, part):
        copy.wait()


def largest_square(rows):
    squares = lax.dot_general(
        jnp.ones((16, HEAD), bf16), rows * rows, rows_rows, preferred_element_type=f32
    )
    return jnp.max(squares)


def add_keys(q, keys, values_t, allowed, first, acc, tot, top, shifted):
    s = lax.dot_general(keys, q, rows_rows, preferred_element_type=f32)
    if allowed is not None:
        few = allowed.shape[1]
        seen = jnp.where(allowed, s[:, :few], masked)
        s = seen if few == s.shape[1] else jnp.concatenate([seen, s[:, few:]], axis=1)
    n, w = s.shape
    s = s * scale2
    if shifted:
        old = top[:, first:]
        new = jnp.maximum(old, jnp.max(s, axis=0, keepdims=True))
        shrink = jnp.exp2(old - new)
        s = s - new
        top[:, first:] = new
        tot[:, first:] = tot[:, first:] * shrink
        acc[:, first:] = acc[:, first:] * shrink
    p = jnp.exp2(s)
    tot[:, first:] += jnp.sum(p.reshape(n // 8, 8, w), axis=0)
    acc[:, first:] += jnp.dot(values_t, p.astype(bf16), preferred_element_type=f32)


def key_block(ks, vt, n, count):
    keys = ks[pl.ds(n, count)].reshape(count * HEAD, HEAD)
    values_t = jnp.concatenate([vt[n + i] for i in range(count)], axis=1)
    return keys, values_t


def either(safe, run):
    @pl.when(safe)
    def _():
        run(False)

    @pl.when(jnp.logical_not(safe))
    def _():
        run(True)


def prompt_kernel(
    k_square_0, k_square_1, q_ref, own_0, got_0, own_1, got_1, o_ref, ks, vt, acc, tot, top, sems
):
    i = pl.program_id(0)
    z = lax.axis_index("z")
    sides = [
        (own, got, ks.at[h], vt.at[h], sems.at[h])
        for h, (own, got) in enumerate(((own_0, got_0), (own_1, got_1)))
    ]

    @pl.when(i == 0)
    def _():
        for part in range(PARTS):
            for side in sides:
                start_keys(part, *side)

    q = q_ref[...].reshape(WIDTH, HEAD)
    k_square = jnp.maximum(k_square_0[0, 0], k_square_1[0, 0])
    safe = largest_square(q) * k_square <= safe_square
    acc[...] = jnp.zeros_like(acc)
    tot[...] = jnp.zeros_like(tot)
    for side in sides:
        wait_keys(i, *side)

    def run(shifted):
        top[...] = jnp.full_like(top, masked if shifted else 0.0)

        def body(t, carry):
            for h in range(2):
                keys, values_t = key_block(ks.at[h], vt.at[h], t * PART, PART)
                add_keys(q, keys, values_t, None, 0, acc, tot, top, shifted)
            return carry

        lax.fori_loop(0, i, body, 0)
        wide = SOME * HEAD
        key = lax.broadcasted_iota(jnp.int32, (wide, wide), 0)
        row = lax.broadcasted_iota(jnp.int32, (1, wide), 1)
        for c in range(PART // SOME):
            keys, values_t = key_block(ks.at[0], vt.at[0], i * PART + c * SOME, SOME)
            add_keys(q[c * wide :], keys, values_t, key <= row, c * wide, acc, tot, top, shifted)

        def others(skip):
            for c in range(PART // SOME - skip):
                first = (c + skip) * wide
                keys, values_t = key_block(ks.at[1], vt.at[1], i * PART + c * SOME, SOME)
                add_keys(q[first:], keys, values_t, None, first, acc, tot, top, shifted)

        @pl.when(z == 1)
        def _():
            others(0)

        @pl.when(z == 0)
        def _():
            others(1)

    either(safe, run)
    total = jnp.sum(tot[...], axis=0, keepdims=True)
    o_ref[...] = (acc[...] / total).T.astype(bf16).reshape(PART, HEAD, HEAD)


def answer_rows(refs):
    rows = jnp.concatenate([ref[...].reshape(-1, 3 * HEAD) for ref in refs], axis=0)
    return rows[:, :HEAD], rows[:, HEAD : 2 * HEAD], rows[:, 2 * HEAD :]


def own_answer_kernel(
    a0, a1, a2, a3, own_ref, got_ref, acc, tot, top, k_square, ks, vt, sems
):
    side = (own_ref, got_ref, ks, vt, sems)
    for part in range(PARTS):
        start_keys(part, *side)
    here = lax.axis_index("x") // 2 == lax.axis_index("z")
    q, near_keys, near_values = answer_rows((a0, a1, a2, a3))
    count = q.shape[0]
    for part in range(PARTS):
        wait_keys(part, *side)
    most = largest_square(ks[...].reshape(-1, HEAD))
    k_square[...] = jnp.full_like(k_square, most)
    acc[...] = jnp.zeros_like(acc)
    tot[...] = jnp.zeros_like(tot)
    top[...] = jnp.zeros_like(top)

    @pl.when(here)
    def _():
        most_near = jnp.maximum(most, largest_square(near_keys))
        safe = largest_square(q) * most_near <= safe_square

        def run(shifted):
            if shifted:
                top[...] = jnp.full_like(top, masked)
            u = lax.broadcasted_iota(jnp.int32, (count, count), 0)
            t = lax.broadcasted_iota(jnp.int32, (1, count), 1)
            allowed = (u >= t - t % 4) & (u <= t)
            add_keys(q, near_keys, near_values.T, allowed, 0, acc, tot, top, shifted)

            def body(part, carry):
                keys, values_t = key_block(ks, vt, part * PART, PART)
                add_keys(q, keys, values_t, None, 0, acc, tot, top, shifted)
                return carry

            lax.fori_loop(0, PARTS, body, 0)

        either(safe, run)


def other_answer_kernel(
    k_square, a0, a1, a2, a3, own_ref, got_ref, acc_in, tot_in, top_in,
    kept_ref, sent_ref, ks, vt, acc, tot, top, sems,
):
    here = lax.axis_index("x") // 2 == lax.axis_index("z")
    side = (own_ref, got_ref, ks, vt, sems)

    @pl.when(jnp.logical_not(here))
    def _():
        kept_ref[...] = jnp.zeros_like(kept_ref)
        sent_ref[...] = jnp.zeros_like(sent_ref)

    @pl.when(here)
    def _():
        for part in range(PARTS):
            start_keys(part, *side)
        q, _, _ = answer_rows((a0, a1, a2, a3))
        acc[...] = acc_in[...]
        tot[...] = tot_in[...]
        top[...] = top_in[...]
        safe = (largest_square(q) * k_square[0, 0] <= safe_square) & (
            jnp.max(jnp.abs(top_in[...])) == 0.0
        )

        def run(shifted):
            def body(part, carry):
                wait_keys(part, *side)
                keys, values_t = key_block(ks, vt, part * PART, PART)
                add_keys(q, keys, values_t, None, 0, acc, tot, top, shifted)
                return carry

            lax.fori_loop(0, PARTS, body, 0)

        either(safe, run)
        total = jnp.sum(tot[...], axis=0, keepdims=True)
        out = (acc[...] / total).T.astype(bf16).reshape(4, 2, -1, HEAD)
        kept_ref[...] = out[:, 0]
        sent_ref[...] = out[:, 1]


def on_device(queries, keys, values, answer_query_rows, answer_key_rows, answer_value_rows):
    params = pltpu.CompilerParams(vmem_limit_bytes=VMEM_LIMIT)
    units = ("x", "core", "y")
    swap = [(0, 1), (1, 0)]
    x, core, z = (lax.axis_index(name) for name in ("x", "core", "z"))
    whole = pl.BlockSpec(memory_space=pltpu.VMEM)
    outside = pl.BlockSpec(memory_space=pltpu.HBM)
    scalars = pl.BlockSpec(memory_space=pltpu.SMEM)
    unit_shape = jax.ShapeDtypeStruct((UNITS, HEAD, HEAD), bf16)
    answers, steps = answer_query_rows.shape[:2]
    rows = answers * steps

    def move(array, axis, by):
        return lax.ppermute(array, axis, [(r, (r + by) % 4) for r in range(4)])

    packed_keys = pl.pallas_call(
        pack_keys_kernel,
        out_shape=unit_shape,
        grid=(2,),
        in_specs=[pl.BlockSpec((HEAD, 8 * HEAD), lambda i: (0, i))] * 2,
        out_specs=pl.BlockSpec((UNITS // 2, HEAD, HEAD), lambda i: (i, 0, 0)),
        compiler_params=params,
    )(keys, values)
    near_shape = jax.ShapeDtypeStruct((2, rows, 3 * HEAD), bf16)
    packed_queries, kept, sent = pl.pallas_call(
        pack_queries_kernel,
        out_shape=(unit_shape, near_shape, near_shape),
        in_specs=[whole] * 4,
        out_specs=(whole,) * 3,
        compiler_params=params,
        cost_estimate=pl.CostEstimate(flops=0, bytes_accessed=2 << 20, transcendentals=0),
    )(queries, answer_query_rows, answer_key_rows, answer_value_rows)

    mixed = jnp.stack([kept, lax.ppermute(sent, "core", swap)], axis=1)
    same, opposite = mixed[0], mixed[1]
    asked = (same, move(opposite, "x", 1), move(same, "x", 2), move(opposite, "x", 3))

    own_0 = lax.all_to_all(packed_keys, units, split_axis=0, concat_axis=0, tiled=True)
    own_0, packed_queries, *asked = lax.optimization_barrier((own_0, packed_queries, *asked))
    own_1 = lax.ppermute(own_0, "z", swap)
    got_0 = lax.ppermute(own_0, "core", swap)
    head_queries = lax.all_to_all(packed_queries, units, split_axis=0, concat_axis=0, tiled=True)

    key_scratch = [pltpu.VMEM((UNITS, HEAD, HEAD), bf16)] * 2
    key_sems = [pltpu.SemaphoreType.DMA((2, PARTS))]
    state_sizes = (HEAD, 8, 1)
    *state, k_square = pl.pallas_call(
        own_answer_kernel,
        out_shape=tuple(jax.ShapeDtypeStruct((n, 8 * rows), f32) for n in state_sizes)
        + (jax.ShapeDtypeStruct((8, HEAD), f32),),
        in_specs=[whole] * 4 + [outside] * 2,
        out_specs=(whole,) * 4,
        scratch_shapes=key_scratch + key_sems,
        compiler_params=params,
        cost_estimate=pl.CostEstimate(flops=5 << 30, bytes_accessed=2 << 20, transcendentals=1 << 21),
    )(*asked, own_0, got_0)
    k_square_1 = lax.ppermute(k_square, "z", swap)
    own_1, k_square_1, head_queries = lax.optimization_barrier((own_1, k_square_1, head_queries))
    got_1 = lax.ppermute(own_1, "core", swap)

    pairs = UNITS * HEAD * 2 * UNITS * HEAD // 2
    attended = pl.pallas_call(
        prompt_kernel,
        out_shape=unit_shape,
        grid=(PARTS,),
        in_specs=[scalars, scalars, pl.BlockSpec((PART, HEAD, HEAD), lambda i: (i, 0, 0))]
        + [outside] * 4,
        out_specs=pl.BlockSpec((PART, HEAD, HEAD), lambda i: (i, 0, 0)),
        scratch_shapes=[pltpu.VMEM((2, UNITS, HEAD, HEAD), bf16)] * 2
        + [pltpu.VMEM((n, WIDTH), f32) for n in state_sizes]
        + [pltpu.SemaphoreType.DMA((2, 2, PARTS))],
        compiler_params=params,
        cost_estimate=pl.CostEstimate(
            flops=8 * HEAD * pairs, bytes_accessed=6 << 20, transcendentals=pairs
        ),
    )(k_square, k_square_1, head_queries, own_0, got_0, own_1, got_1)
    returned = lax.all_to_all(attended, units, split_axis=0, concat_axis=0, tiled=True)

    state = lax.optimization_barrier((attended, *state))[1:]
    answer_shape = jax.ShapeDtypeStruct((4, rows, HEAD), bf16)
    kept, sent = pl.pallas_call(
        other_answer_kernel,
        out_shape=(answer_shape, answer_shape),
        in_specs=[scalars] + [whole] * 4 + [outside] * 2 + [whole] * 3,
        out_specs=(whole, whole),
        scratch_shapes=key_scratch
        + [pltpu.VMEM((n, 8 * rows), f32) for n in state_sizes]
        + key_sems,
        compiler_params=params,
        cost_estimate=pl.CostEstimate(flops=5 << 30, bytes_accessed=2 << 20, transcendentals=1 << 21),
    )(k_square_1, *asked, own_1, got_1, *state)
    back = lax.ppermute(sent, "core", swap)
    pair = jnp.concatenate(
        [jnp.where(core == 0, kept, back), jnp.where(core == 0, back, kept)], axis=-1
    )
    four = jnp.stack([pair[0]] + [move(pair[by], "x", -by) for by in (1, 2, 3)])
    answer_out = jnp.concatenate(
        [lax.dynamic_index_in_dim(four, (2 * z + p - x) % 4, 0, False) for p in range(2)],
        axis=-1,
    ).reshape(answers, steps, 4 * HEAD)

    prefill_out = pl.pallas_call(
        unpack_kernel,
        out_shape=jax.ShapeDtypeStruct((HEAD, UNITS * HEAD), bf16),
        grid=(2,),
        in_specs=[pl.BlockSpec((UNITS // 2, HEAD, HEAD), lambda i: (i, 0, 0))],
        out_specs=pl.BlockSpec((HEAD, 16 * HEAD), lambda i: (0, i)),
        compiler_params=params,
    )(returned)
    return prefill_out, answer_out


def solution(mesh):
    fine = Mesh(mesh.devices.reshape(4, 2, 2, 4, 4), ("x", "core", "z", "y", "prompt"))
    tokens = P(("prompt", "x", "core", "z", "y"), None)
    rows = P(("prompt", "x", "core"), None, ("z", "y"))
    return jax.shard_map(
        on_device,
        mesh=fine,
        in_specs=(tokens, tokens, tokens, rows, rows, rows),
        out_specs=(tokens, rows),
        check_vma=False,
    )
```

```python
import math

import jax
import jax.numpy as jnp
from jax import lax
from jax.experimental import pallas as pl
from jax.experimental.pallas import tpu as pltpu
from jax.sharding import Mesh, PartitionSpec as P


HEAD = 128
score_scale = 168.0 ** (-0.5)
scale2 = score_scale * math.log2(math.e)
masked = -1e30
safe_square = (100.0 / scale2) ** 2
VMEM_LIMIT = 66500000
bf16, f32 = jnp.bfloat16, jnp.float32
rows_rows = (((1,), (1,)), ((), ()))

UNITS = 32
SOME = 4
PART = 8
WIDTH = PART * HEAD
PARTS = UNITS // PART


def half_heads():
    return [
        ((2 * p + core) * 4 + y, 2 * y + p, core)
        for p in range(2)
        for core in range(2)
        for y in range(4)
    ]


def pack_keys_kernel(k_ref, v_ref, out_ref):
    for to, g, core in half_heads():
        at = g * HEAD
        if core == 0:
            out_ref[to] = k_ref[:, at : at + HEAD]
        else:
            out_ref[to] = v_ref[:, at : at + HEAD].T


def pack_queries_kernel(q_ref, out_ref):
    for to, g, core in half_heads():
        at = (2 * g + core) * HEAD
        out_ref[to] = q_ref[:, at : at + HEAD]


def pack_answers_kernel(aq_ref, ak_ref, av_ref, kept_ref, sent_ref):
    odd = lax.axis_index("x") % 2
    here = lax.axis_index("core")
    rows = kept_ref.shape[1]
    q_rows = aq_ref[...].reshape(rows, 4 * HEAD)
    k_rows = ak_ref[...].reshape(rows, 2 * HEAD)
    v_rows = av_ref[...].reshape(rows, 2 * HEAD)
    for p in range(2):
        at = (odd + p) % 2
        near = [rows_of[:, p * HEAD : (p + 1) * HEAD] for rows_of in (k_rows, v_rows)]
        both = [q_rows[:, (2 * p + core) * HEAD : (2 * p + core + 1) * HEAD] for core in range(2)]
        for to_ref, mine in ((kept_ref, here == 0), (sent_ref, here == 1)):
            to_ref[at] = jnp.concatenate([jnp.where(mine, both[0], both[1]), *near], axis=1)


def unpack_kernel(in_ref, out_ref):
    for place, g, core in half_heads():
        at = (2 * g + core) * HEAD
        out_ref[:, at : at + HEAD] = in_ref[place]


def copies(core, own_ref, got_ref, ks, vt, sems, part):
    at = pl.ds(part * PART, PART)
    key_ref, value_ref = (own_ref, got_ref) if core == 0 else (got_ref, own_ref)
    return (
        pltpu.make_async_copy(key_ref.at[at], ks.at[at], sems.at[0, part]),
        pltpu.make_async_copy(value_ref.at[at], vt.at[at], sems.at[1, part]),
    )


def start_keys(part, *refs):
    here = lax.axis_index("core")
    for core in range(2):

        @pl.when(here == core)
        def _():
            for copy in copies(core, *refs, part):
                copy.start()


def wait_keys(part, *refs):
    for copy in copies(0, *refs, part):
        copy.wait()


def largest_square(rows):
    squares = lax.dot_general(
        jnp.ones((16, HEAD), bf16), rows * rows, rows_rows, preferred_element_type=f32
    )
    return jnp.max(squares)


def add_keys(q, keys, values_t, allowed, first, acc, tot, top, shifted):
    s = lax.dot_general(keys, q, rows_rows, preferred_element_type=f32)
    if allowed is not None:
        few = allowed.shape[1]
        seen = jnp.where(allowed, s[:, :few], masked)
        s = seen if few == s.shape[1] else jnp.concatenate([seen, s[:, few:]], axis=1)
    n, w = s.shape
    s = s * scale2
    if shifted:
        old = top[:, first:]
        new = jnp.maximum(old, jnp.max(s, axis=0, keepdims=True))
        shrink = jnp.exp2(old - new)
        s = s - new
        top[:, first:] = new
        tot[:, first:] = tot[:, first:] * shrink
        acc[:, first:] = acc[:, first:] * shrink
    p = jnp.exp2(s)
    tot[:, first:] += jnp.sum(p.reshape(n // 8, 8, w), axis=0)
    acc[:, first:] += jnp.dot(values_t, p.astype(bf16), preferred_element_type=f32)


def key_block(ks, vt, n, count):
    keys = ks[pl.ds(n, count)].reshape(count * HEAD, HEAD)
    values_t = jnp.concatenate([vt[n + i] for i in range(count)], axis=1)
    return keys, values_t


def either(safe, run):
    @pl.when(safe)
    def _():
        run(False)

    @pl.when(jnp.logical_not(safe))
    def _():
        run(True)


def prompt_kernel(
    k_square_0, k_square_1, q_ref, own_0, got_0, own_1, got_1, o_ref, ks, vt, acc, tot, top, sems
):
    i = pl.program_id(0)
    z = lax.axis_index("z")
    sides = [
        (own, got, ks.at[h], vt.at[h], sems.at[h])
        for h, (own, got) in enumerate(((own_0, got_0), (own_1, got_1)))
    ]

    @pl.when(i == 0)
    def _():
        for part in range(PARTS):
            for side in sides:
                start_keys(part, *side)

    q = q_ref[...].reshape(WIDTH, HEAD)
    k_square = jnp.maximum(k_square_0[0, 0], k_square_1[0, 0])
    safe = largest_square(q) * k_square <= safe_square
    acc[...] = jnp.zeros_like(acc)
    tot[...] = jnp.zeros_like(tot)
    for side in sides:
        wait_keys(i, *side)

    def run(shifted):
        top[...] = jnp.full_like(top, masked if shifted else 0.0)

        def body(t, carry):
            blocks = [key_block(ks.at[h], vt.at[h], t * PART, PART) for h in range(2)]
            keys = jnp.concatenate([k for k, _ in blocks], axis=0)
            values_t = jnp.concatenate([v for _, v in blocks], axis=1)
            add_keys(q, keys, values_t, None, 0, acc, tot, top, shifted)
            return carry

        lax.fori_loop(0, i, body, 0)
        wide = SOME * HEAD
        key = lax.broadcasted_iota(jnp.int32, (2 * wide, wide), 0)
        row = lax.broadcasted_iota(jnp.int32, (1, wide), 1)
        allowed = (key <= row) | (key >= wide)

        def diagonal(skip):
            for c in range(PART // SOME):
                blocks = [key_block(ks.at[0], vt.at[0], i * PART + c * SOME, SOME)]
                if c >= skip:
                    at = i * PART + (c - skip) * SOME
                    blocks.append(key_block(ks.at[1], vt.at[1], at, SOME))
                keys = jnp.concatenate([k for k, _ in blocks], axis=0)
                values_t = jnp.concatenate([v for _, v in blocks], axis=1)
                first = c * wide
                add_keys(
                    q[first:], keys, values_t, allowed[: len(blocks) * wide], first,
                    acc, tot, top, shifted,
                )

        @pl.when(z == 1)
        def _():
            diagonal(0)

        @pl.when(z == 0)
        def _():
            diagonal(1)

    either(safe, run)
    total = jnp.sum(tot[...], axis=0, keepdims=True)
    o_ref[...] = (acc[...] / total).T.astype(bf16).reshape(PART, HEAD, HEAD)


def answer_rows(refs):
    rows = jnp.concatenate([ref[...].reshape(-1, 3 * HEAD) for ref in refs], axis=0)
    return rows[:, :HEAD], rows[:, HEAD : 2 * HEAD], rows[:, 2 * HEAD :]


def own_answer_kernel(
    a0, a1, a2, a3, own_ref, got_ref, acc, tot, top, k_square, ks, vt, sems
):
    side = (own_ref, got_ref, ks, vt, sems)
    for part in range(PARTS):
        start_keys(part, *side)
    here = lax.axis_index("x") // 2 == lax.axis_index("z")
    q, near_keys, near_values = answer_rows((a0, a1, a2, a3))
    count = q.shape[0]
    for part in range(PARTS):
        wait_keys(part, *side)
    most = largest_square(ks[...].reshape(-1, HEAD))
    k_square[...] = jnp.full_like(k_square, most)
    acc[...] = jnp.zeros_like(acc)
    tot[...] = jnp.zeros_like(tot)
    top[...] = jnp.zeros_like(top)

    @pl.when(here)
    def _():
        most_near = jnp.maximum(most, largest_square(near_keys))
        safe = largest_square(q) * most_near <= safe_square

        def run(shifted):
            if shifted:
                top[...] = jnp.full_like(top, masked)
            u = lax.broadcasted_iota(jnp.int32, (count, count), 0)
            t = lax.broadcasted_iota(jnp.int32, (1, count), 1)
            allowed = (u >= t - t % 4) & (u <= t)
            add_keys(q, near_keys, near_values.T, allowed, 0, acc, tot, top, shifted)

            def body(part, carry):
                keys, values_t = key_block(ks, vt, part * PART, PART)
                add_keys(q, keys, values_t, None, 0, acc, tot, top, shifted)
                return carry

            lax.fori_loop(0, PARTS, body, 0)

        either(safe, run)


def other_answer_kernel(
    k_square, a0, a1, a2, a3, own_ref, got_ref, acc_in, tot_in, top_in,
    kept_ref, sent_ref, ks, vt, acc, tot, top, sems,
):
    here = lax.axis_index("x") // 2 == lax.axis_index("z")
    side = (own_ref, got_ref, ks, vt, sems)

    @pl.when(jnp.logical_not(here))
    def _():
        kept_ref[...] = jnp.zeros_like(kept_ref)
        sent_ref[...] = jnp.zeros_like(sent_ref)

    @pl.when(here)
    def _():
        for part in range(PARTS):
            start_keys(part, *side)
        q, _, _ = answer_rows((a0, a1, a2, a3))
        acc[...] = acc_in[...]
        tot[...] = tot_in[...]
        top[...] = top_in[...]
        safe = (largest_square(q) * k_square[0, 0] <= safe_square) & (
            jnp.max(jnp.abs(top_in[...])) == 0.0
        )

        def run(shifted):
            def body(part, carry):
                wait_keys(part, *side)
                keys, values_t = key_block(ks, vt, part * PART, PART)
                add_keys(q, keys, values_t, None, 0, acc, tot, top, shifted)
                return carry

            lax.fori_loop(0, PARTS, body, 0)

        either(safe, run)
        total = jnp.sum(tot[...], axis=0, keepdims=True)
        out = (acc[...] / total).T.astype(bf16).reshape(4, 2, -1, HEAD)
        kept_ref[...] = out[:, 0]
        sent_ref[...] = out[:, 1]


def on_device(queries, keys, values, answer_query_rows, answer_key_rows, answer_value_rows):
    params = pltpu.CompilerParams(vmem_limit_bytes=VMEM_LIMIT)
    units = ("x", "core", "y")
    swap = [(0, 1), (1, 0)]
    x, core, z = (lax.axis_index(name) for name in ("x", "core", "z"))
    whole = pl.BlockSpec(memory_space=pltpu.VMEM)
    outside = pl.BlockSpec(memory_space=pltpu.HBM)
    scalars = pl.BlockSpec(memory_space=pltpu.SMEM)
    unit_shape = jax.ShapeDtypeStruct((UNITS, HEAD, HEAD), bf16)
    answers, steps = answer_query_rows.shape[:2]
    rows = answers * steps

    def move(array, axis, by):
        return lax.ppermute(array, axis, [(r, (r + by) % 4) for r in range(4)])

    packed_keys = pl.pallas_call(
        pack_keys_kernel,
        out_shape=unit_shape,
        grid=(2,),
        in_specs=[pl.BlockSpec((HEAD, 8 * HEAD), lambda i: (0, i))] * 2,
        out_specs=pl.BlockSpec((UNITS // 2, HEAD, HEAD), lambda i: (i, 0, 0)),
        compiler_params=params,
    )(keys, values)
    near_shape = jax.ShapeDtypeStruct((2, rows, 3 * HEAD), bf16)
    kept, sent = pl.pallas_call(
        pack_answers_kernel,
        out_shape=(near_shape, near_shape),
        in_specs=[whole] * 3,
        out_specs=(whole,) * 2,
        compiler_params=params,
        cost_estimate=pl.CostEstimate(flops=0, bytes_accessed=1 << 18, transcendentals=0),
    )(answer_query_rows, answer_key_rows, answer_value_rows)
    packed_queries = pl.pallas_call(
        pack_queries_kernel,
        out_shape=unit_shape,
        grid=(2,),
        in_specs=[pl.BlockSpec((HEAD, 16 * HEAD), lambda i: (0, i))],
        out_specs=pl.BlockSpec((UNITS // 2, HEAD, HEAD), lambda i: (i, 0, 0)),
        compiler_params=params,
        cost_estimate=pl.CostEstimate(flops=0, bytes_accessed=2 << 20, transcendentals=0),
    )(queries)

    mixed = jnp.stack([kept, lax.ppermute(sent, "core", swap)], axis=1)
    same, opposite = mixed[0], mixed[1]
    asked = (same, move(opposite, "x", 1), move(same, "x", 2), move(opposite, "x", 3))

    own_0 = lax.all_to_all(packed_keys, units, split_axis=0, concat_axis=0, tiled=True)
    own_0, packed_queries, *asked = lax.optimization_barrier((own_0, packed_queries, *asked))
    own_1 = lax.ppermute(own_0, "z", swap)
    got_0 = lax.ppermute(own_0, "core", swap)
    head_queries = lax.all_to_all(packed_queries, units, split_axis=0, concat_axis=0, tiled=True)

    key_scratch = [pltpu.VMEM((UNITS, HEAD, HEAD), bf16)] * 2
    key_sems = [pltpu.SemaphoreType.DMA((2, PARTS))]
    state_sizes = (HEAD, 8, 1)
    *state, k_square = pl.pallas_call(
        own_answer_kernel,
        out_shape=tuple(jax.ShapeDtypeStruct((n, 8 * rows), f32) for n in state_sizes)
        + (jax.ShapeDtypeStruct((8, HEAD), f32),),
        in_specs=[whole] * 4 + [outside] * 2,
        out_specs=(whole,) * 4,
        scratch_shapes=key_scratch + key_sems,
        compiler_params=params,
        cost_estimate=pl.CostEstimate(flops=5 << 30, bytes_accessed=2 << 20, transcendentals=1 << 21),
    )(*asked, own_0, got_0)
    k_square_1 = lax.ppermute(k_square, "z", swap)
    own_1, k_square_1, head_queries = lax.optimization_barrier((own_1, k_square_1, head_queries))
    got_1 = lax.ppermute(own_1, "core", swap)

    pairs = UNITS * HEAD * 2 * UNITS * HEAD // 2
    attended = pl.pallas_call(
        prompt_kernel,
        out_shape=unit_shape,
        grid=(PARTS,),
        in_specs=[scalars, scalars, pl.BlockSpec((PART, HEAD, HEAD), lambda i: (i, 0, 0))]
        + [outside] * 4,
        out_specs=pl.BlockSpec((PART, HEAD, HEAD), lambda i: (i, 0, 0)),
        scratch_shapes=[pltpu.VMEM((2, UNITS, HEAD, HEAD), bf16)] * 2
        + [pltpu.VMEM((n, WIDTH), f32) for n in state_sizes]
        + [pltpu.SemaphoreType.DMA((2, 2, PARTS))],
        compiler_params=params,
        cost_estimate=pl.CostEstimate(
            flops=8 * HEAD * pairs, bytes_accessed=6 << 20, transcendentals=pairs
        ),
    )(k_square, k_square_1, head_queries, own_0, got_0, own_1, got_1)
    returned = lax.all_to_all(attended, units, split_axis=0, concat_axis=0, tiled=True)

    state = lax.optimization_barrier((attended, *state))[1:]
    answer_shape = jax.ShapeDtypeStruct((4, rows, HEAD), bf16)
    kept, sent = pl.pallas_call(
        other_answer_kernel,
        out_shape=(answer_shape, answer_shape),
        in_specs=[scalars] + [whole] * 4 + [outside] * 2 + [whole] * 3,
        out_specs=(whole, whole),
        scratch_shapes=key_scratch
        + [pltpu.VMEM((n, 8 * rows), f32) for n in state_sizes]
        + key_sems,
        compiler_params=params,
        cost_estimate=pl.CostEstimate(flops=5 << 30, bytes_accessed=2 << 20, transcendentals=1 << 21),
    )(k_square_1, *asked, own_1, got_1, *state)
    back = lax.ppermute(sent, "core", swap)
    pair = jnp.concatenate(
        [jnp.where(core == 0, kept, back), jnp.where(core == 0, back, kept)], axis=-1
    )
    four = jnp.stack([pair[0]] + [move(pair[by], "x", -by) for by in (1, 2, 3)])
    answer_out = jnp.concatenate(
        [lax.dynamic_index_in_dim(four, (2 * z + p - x) % 4, 0, False) for p in range(2)],
        axis=-1,
    ).reshape(answers, steps, 4 * HEAD)

    prefill_out = pl.pallas_call(
        unpack_kernel,
        out_shape=jax.ShapeDtypeStruct((HEAD, UNITS * HEAD), bf16),
        grid=(2,),
        in_specs=[pl.BlockSpec((UNITS // 2, HEAD, HEAD), lambda i: (i, 0, 0))],
        out_specs=pl.BlockSpec((HEAD, 16 * HEAD), lambda i: (0, i)),
        compiler_params=params,
    )(returned)
    return prefill_out, answer_out


def solution(mesh):
    fine = Mesh(mesh.devices.reshape(4, 2, 2, 4, 4), ("x", "core", "z", "y", "prompt"))
    tokens = P(("prompt", "x", "core", "z", "y"), None)
    rows = P(("prompt", "x", "core"), None, ("z", "y"))
    return jax.shard_map(
        on_device,
        mesh=fine,
        in_specs=(tokens, tokens, tokens, rows, rows, rows),
        out_specs=(tokens, rows),
        check_vma=False,
    )
```

```python
import math

import jax
import jax.numpy as jnp
from jax import lax
from jax.experimental import pallas as pl
from jax.experimental.pallas import tpu as pltpu
from jax.sharding import Mesh, PartitionSpec as P


HEAD = 128
score_scale = 168.0 ** (-0.5)
scale2 = score_scale * math.log2(math.e)
masked = -1e30
safe_square = (100.0 / scale2) ** 2
VMEM_LIMIT = 66500000
bf16, f32 = jnp.bfloat16, jnp.float32
rows_rows = (((1,), (1,)), ((), ()))

UNITS = 32
SOME = 4
PART = 8
WIDTH = PART * HEAD
PARTS = UNITS // PART


def half_heads():
    return [
        ((2 * p + core) * 4 + y, 2 * y + p, core)
        for p in range(2)
        for core in range(2)
        for y in range(4)
    ]


def pack_keys_kernel(k_ref, v_ref, out_ref):
    for to, g, core in half_heads():
        at = g * HEAD
        if core == 0:
            out_ref[to] = k_ref[:, at : at + HEAD]
        else:
            out_ref[to] = v_ref[:, at : at + HEAD].T


def pack_queries_kernel(q_ref, out_ref):
    for to, g, core in half_heads():
        at = (2 * g + core) * HEAD
        out_ref[to] = q_ref[:, at : at + HEAD]


def pack_answers_kernel(aq_ref, ak_ref, av_ref, kept_ref, sent_ref):
    odd = lax.axis_index("x") % 2
    here = lax.axis_index("core")
    rows = kept_ref.shape[1]
    q_rows = aq_ref[...].reshape(rows, 4 * HEAD)
    k_rows = ak_ref[...].reshape(rows, 2 * HEAD)
    v_rows = av_ref[...].reshape(rows, 2 * HEAD)
    for p in range(2):
        at = (odd + p) % 2
        near = [rows_of[:, p * HEAD : (p + 1) * HEAD] for rows_of in (k_rows, v_rows)]
        both = [q_rows[:, (2 * p + core) * HEAD : (2 * p + core + 1) * HEAD] for core in range(2)]
        for to_ref, mine in ((kept_ref, here == 0), (sent_ref, here == 1)):
            to_ref[at] = jnp.concatenate([jnp.where(mine, both[0], both[1]), *near], axis=1)


def unpack_kernel(in_ref, out_ref):
    for place, g, core in half_heads():
        at = (2 * g + core) * HEAD
        out_ref[:, at : at + HEAD] = in_ref[place]


def copies(core, own_ref, got_ref, ks, vt, sems, part):
    at = pl.ds(part * PART, PART)
    key_ref, value_ref = (own_ref, got_ref) if core == 0 else (got_ref, own_ref)
    return (
        pltpu.make_async_copy(key_ref.at[at], ks.at[at], sems.at[0, part]),
        pltpu.make_async_copy(value_ref.at[at], vt.at[at], sems.at[1, part]),
    )


def start_keys(part, *refs):
    here = lax.axis_index("core")
    for core in range(2):

        @pl.when(here == core)
        def _():
            for copy in copies(core, *refs, part):
                copy.start()


def wait_keys(part, *refs):
    for copy in copies(0, *refs, part):
        copy.wait()


def largest_square(rows):
    squares = lax.dot_general(
        jnp.ones((16, HEAD), bf16), rows * rows, rows_rows, preferred_element_type=f32
    )
    return jnp.max(squares)


def add_keys(q, keys, values_t, allowed, first, acc, tot, top, shifted):
    s = lax.dot_general(keys, q, rows_rows, preferred_element_type=f32)
    if allowed is not None:
        few = allowed.shape[1]
        seen = jnp.where(allowed, s[:, :few], masked)
        s = seen if few == s.shape[1] else jnp.concatenate([seen, s[:, few:]], axis=1)
    n, w = s.shape
    s = s * scale2
    if shifted:
        old = top[:, first:]
        new = jnp.maximum(old, jnp.max(s, axis=0, keepdims=True))
        shrink = jnp.exp2(old - new)
        s = s - new
        top[:, first:] = new
        tot[:, first:] = tot[:, first:] * shrink
        acc[:, first:] = acc[:, first:] * shrink
    p = jnp.exp2(s)
    tot[:, first:] += jnp.sum(p.reshape(n // 8, 8, w), axis=0)
    acc[:, first:] += jnp.dot(values_t, p.astype(bf16), preferred_element_type=f32)


def key_block(ks, vt, n, count):
    keys = ks[pl.ds(n, count)].reshape(count * HEAD, HEAD)
    values_t = jnp.concatenate([vt[n + i] for i in range(count)], axis=1)
    return keys, values_t


def either(safe, run):
    @pl.when(safe)
    def _():
        run(False)

    @pl.when(jnp.logical_not(safe))
    def _():
        run(True)


def square_kernel(q_ref, square_ref):
    square_ref[...] = jnp.full_like(square_ref, largest_square(q_ref[...].reshape(-1, HEAD)))


def prompt_kernel(
    q_square, k_square_0, k_square_1, q_ref, own_0, got_0, own_1, got_1, o_ref, ks, vt, acc, tot, top, sems
):
    i = pl.program_id(0)
    z = lax.axis_index("z")
    sides = [
        (own, got, ks.at[h], vt.at[h], sems.at[h])
        for h, (own, got) in enumerate(((own_0, got_0), (own_1, got_1)))
    ]

    @pl.when(i == 0)
    def _():
        for part in range(PARTS):
            for side in sides:
                start_keys(part, *side)

    q = q_ref[...].reshape(WIDTH, HEAD)
    k_square = jnp.maximum(k_square_0[0, 0], k_square_1[0, 0])
    safe = q_square[0, 0] * k_square <= safe_square
    acc[...] = jnp.zeros_like(acc)
    tot[...] = jnp.zeros_like(tot)
    for side in sides:
        wait_keys(i, *side)

    def run(shifted):
        top[...] = jnp.full_like(top, masked if shifted else 0.0)

        def body(t, carry):
            blocks = [key_block(ks.at[h], vt.at[h], t * PART, PART) for h in range(2)]
            keys = jnp.concatenate([k for k, _ in blocks], axis=0)
            values_t = jnp.concatenate([v for _, v in blocks], axis=1)
            add_keys(q, keys, values_t, None, 0, acc, tot, top, shifted)
            return carry

        lax.fori_loop(0, i, body, 0)
        wide = SOME * HEAD
        key = lax.broadcasted_iota(jnp.int32, (2 * wide, wide), 0)
        row = lax.broadcasted_iota(jnp.int32, (1, wide), 1)
        allowed = (key <= row) | (key >= wide)

        def diagonal(skip):
            for c in range(PART // SOME):
                blocks = [key_block(ks.at[0], vt.at[0], i * PART + c * SOME, SOME)]
                if c >= skip:
                    at = i * PART + (c - skip) * SOME
                    blocks.append(key_block(ks.at[1], vt.at[1], at, SOME))
                keys = jnp.concatenate([k for k, _ in blocks], axis=0)
                values_t = jnp.concatenate([v for _, v in blocks], axis=1)
                first = c * wide
                add_keys(
                    q[first:], keys, values_t, allowed[: len(blocks) * wide], first,
                    acc, tot, top, shifted,
                )

        @pl.when(z == 1)
        def _():
            diagonal(0)

        @pl.when(z == 0)
        def _():
            diagonal(1)

    either(safe, run)
    total = jnp.sum(tot[...], axis=0, keepdims=True)
    o_ref[...] = (acc[...] * (1.0 / total)).astype(bf16).T.reshape(PART, HEAD, HEAD)


def answer_rows(refs):
    rows = jnp.concatenate([ref[...].reshape(-1, 3 * HEAD) for ref in refs], axis=0)
    return rows[:, :HEAD], rows[:, HEAD : 2 * HEAD], rows[:, 2 * HEAD :]


def own_answer_kernel(
    a0, a1, a2, a3, own_ref, got_ref, acc, tot, top, k_square, ks, vt, sems
):
    side = (own_ref, got_ref, ks, vt, sems)
    for part in range(PARTS):
        start_keys(part, *side)
    here = lax.axis_index("x") // 2 == lax.axis_index("z")
    q, near_keys, near_values = answer_rows((a0, a1, a2, a3))
    count = q.shape[0]
    for part in range(PARTS):
        wait_keys(part, *side)
    most = largest_square(ks[...].reshape(-1, HEAD))
    k_square[...] = jnp.full_like(k_square, most)
    acc[...] = jnp.zeros_like(acc)
    tot[...] = jnp.zeros_like(tot)
    top[...] = jnp.zeros_like(top)

    @pl.when(here)
    def _():
        most_near = jnp.maximum(most, largest_square(near_keys))
        safe = largest_square(q) * most_near <= safe_square

        def run(shifted):
            if shifted:
                top[...] = jnp.full_like(top, masked)
            u = lax.broadcasted_iota(jnp.int32, (count, count), 0)
            t = lax.broadcasted_iota(jnp.int32, (1, count), 1)
            allowed = (u >= t - t % 4) & (u <= t)
            add_keys(q, near_keys, near_values.T, allowed, 0, acc, tot, top, shifted)

            def body(part, carry):
                keys, values_t = key_block(ks, vt, part * PART, PART)
                add_keys(q, keys, values_t, None, 0, acc, tot, top, shifted)
                return carry

            lax.fori_loop(0, PARTS, body, 0)

        either(safe, run)


def other_answer_kernel(
    k_square, a0, a1, a2, a3, own_ref, got_ref, acc_in, tot_in, top_in,
    kept_ref, sent_ref, ks, vt, acc, tot, top, sems,
):
    here = lax.axis_index("x") // 2 == lax.axis_index("z")
    side = (own_ref, got_ref, ks, vt, sems)

    @pl.when(jnp.logical_not(here))
    def _():
        kept_ref[...] = jnp.zeros_like(kept_ref)
        sent_ref[...] = jnp.zeros_like(sent_ref)

    @pl.when(here)
    def _():
        for part in range(PARTS):
            start_keys(part, *side)
        q, _, _ = answer_rows((a0, a1, a2, a3))
        acc[...] = acc_in[...]
        tot[...] = tot_in[...]
        top[...] = top_in[...]
        safe = (largest_square(q) * k_square[0, 0] <= safe_square) & (
            jnp.max(jnp.abs(top_in[...])) == 0.0
        )

        def run(shifted):
            def body(part, carry):
                wait_keys(part, *side)
                keys, values_t = key_block(ks, vt, part * PART, PART)
                add_keys(q, keys, values_t, None, 0, acc, tot, top, shifted)
                return carry

            lax.fori_loop(0, PARTS, body, 0)

        either(safe, run)
        total = jnp.sum(tot[...], axis=0, keepdims=True)
        out = (acc[...] * (1.0 / total)).astype(bf16).T.reshape(4, 2, -1, HEAD)
        kept_ref[...] = out[:, 0]
        sent_ref[...] = out[:, 1]


def on_device(queries, keys, values, answer_query_rows, answer_key_rows, answer_value_rows):
    params = pltpu.CompilerParams(vmem_limit_bytes=VMEM_LIMIT)
    units = ("x", "core", "y")
    swap = [(0, 1), (1, 0)]
    x, core, z = (lax.axis_index(name) for name in ("x", "core", "z"))
    whole = pl.BlockSpec(memory_space=pltpu.VMEM)
    outside = pl.BlockSpec(memory_space=pltpu.HBM)
    scalars = pl.BlockSpec(memory_space=pltpu.SMEM)
    unit_shape = jax.ShapeDtypeStruct((UNITS, HEAD, HEAD), bf16)
    answers, steps = answer_query_rows.shape[:2]
    rows = answers * steps

    def move(array, axis, by):
        return lax.ppermute(array, axis, [(r, (r + by) % 4) for r in range(4)])

    packed_keys = pl.pallas_call(
        pack_keys_kernel,
        out_shape=unit_shape,
        grid=(2,),
        in_specs=[pl.BlockSpec((HEAD, 8 * HEAD), lambda i: (0, i))] * 2,
        out_specs=pl.BlockSpec((UNITS // 2, HEAD, HEAD), lambda i: (i, 0, 0)),
        compiler_params=params,
    )(keys, values)
    near_shape = jax.ShapeDtypeStruct((2, rows, 3 * HEAD), bf16)
    kept, sent = pl.pallas_call(
        pack_answers_kernel,
        out_shape=(near_shape, near_shape),
        in_specs=[whole] * 3,
        out_specs=(whole,) * 2,
        compiler_params=params,
        cost_estimate=pl.CostEstimate(flops=0, bytes_accessed=1 << 18, transcendentals=0),
    )(answer_query_rows, answer_key_rows, answer_value_rows)
    packed_queries = pl.pallas_call(
        pack_queries_kernel,
        out_shape=unit_shape,
        grid=(2,),
        in_specs=[pl.BlockSpec((HEAD, 16 * HEAD), lambda i: (0, i))],
        out_specs=pl.BlockSpec((UNITS // 2, HEAD, HEAD), lambda i: (i, 0, 0)),
        compiler_params=params,
        cost_estimate=pl.CostEstimate(flops=0, bytes_accessed=2 << 20, transcendentals=0),
    )(queries)

    mixed = jnp.stack([kept, lax.ppermute(sent, "core", swap)], axis=1)
    same, opposite = mixed[0], mixed[1]
    asked = (same, move(opposite, "x", 1), move(same, "x", 2), move(opposite, "x", 3))

    own_0 = lax.all_to_all(packed_keys, units, split_axis=0, concat_axis=0, tiled=True)
    own_0, packed_queries, *asked = lax.optimization_barrier((own_0, packed_queries, *asked))
    own_1 = lax.ppermute(own_0, "z", swap)
    got_0 = lax.ppermute(own_0, "core", swap)
    head_queries = lax.all_to_all(packed_queries, units, split_axis=0, concat_axis=0, tiled=True)

    key_scratch = [pltpu.VMEM((UNITS, HEAD, HEAD), bf16)] * 2
    key_sems = [pltpu.SemaphoreType.DMA((2, PARTS))]
    state_sizes = (HEAD, 8, 1)
    *state, k_square = pl.pallas_call(
        own_answer_kernel,
        out_shape=tuple(jax.ShapeDtypeStruct((n, 8 * rows), f32) for n in state_sizes)
        + (jax.ShapeDtypeStruct((8, HEAD), f32),),
        in_specs=[whole] * 4 + [outside] * 2,
        out_specs=(whole,) * 4,
        scratch_shapes=key_scratch + key_sems,
        compiler_params=params,
        cost_estimate=pl.CostEstimate(flops=5 << 30, bytes_accessed=2 << 20, transcendentals=1 << 21),
    )(*asked, own_0, got_0)
    k_square_1 = lax.ppermute(k_square, "z", swap)
    own_1, k_square_1, head_queries = lax.optimization_barrier((own_1, k_square_1, head_queries))
    got_1 = lax.ppermute(own_1, "core", swap)

    q_square = pl.pallas_call(
        square_kernel,
        out_shape=jax.ShapeDtypeStruct((8, HEAD), f32),
        in_specs=[whole],
        out_specs=whole,
        compiler_params=params,
        cost_estimate=pl.CostEstimate(flops=1 << 30, bytes_accessed=1 << 20, transcendentals=0),
    )(head_queries)
    pairs = UNITS * HEAD * 2 * UNITS * HEAD // 2
    attended = pl.pallas_call(
        prompt_kernel,
        out_shape=unit_shape,
        grid=(PARTS,),
        in_specs=[scalars] * 3 + [pl.BlockSpec((PART, HEAD, HEAD), lambda i: (i, 0, 0))]
        + [outside] * 4,
        out_specs=pl.BlockSpec((PART, HEAD, HEAD), lambda i: (i, 0, 0)),
        scratch_shapes=[pltpu.VMEM((2, UNITS, HEAD, HEAD), bf16)] * 2
        + [pltpu.VMEM((n, WIDTH), f32) for n in state_sizes]
        + [pltpu.SemaphoreType.DMA((2, 2, PARTS))],
        compiler_params=params,
        cost_estimate=pl.CostEstimate(
            flops=8 * HEAD * pairs, bytes_accessed=6 << 20, transcendentals=pairs
        ),
    )(q_square, k_square, k_square_1, head_queries, own_0, got_0, own_1, got_1)
    returned = lax.all_to_all(attended, units, split_axis=0, concat_axis=0, tiled=True)

    state = lax.optimization_barrier((attended, *state))[1:]
    answer_shape = jax.ShapeDtypeStruct((4, rows, HEAD), bf16)
    kept, sent = pl.pallas_call(
        other_answer_kernel,
        out_shape=(answer_shape, answer_shape),
        in_specs=[scalars] + [whole] * 4 + [outside] * 2 + [whole] * 3,
        out_specs=(whole, whole),
        scratch_shapes=key_scratch
        + [pltpu.VMEM((n, 8 * rows), f32) for n in state_sizes]
        + key_sems,
        compiler_params=params,
        cost_estimate=pl.CostEstimate(flops=5 << 30, bytes_accessed=2 << 20, transcendentals=1 << 21),
    )(k_square_1, *asked, own_1, got_1, *state)
    back = lax.ppermute(sent, "core", swap)
    pair = jnp.concatenate(
        [jnp.where(core == 0, kept, back), jnp.where(core == 0, back, kept)], axis=-1
    )
    four = jnp.stack([pair[0]] + [move(pair[by], "x", -by) for by in (1, 2, 3)])
    answer_out = jnp.concatenate(
        [lax.dynamic_index_in_dim(four, (2 * z + p - x) % 4, 0, False) for p in range(2)],
        axis=-1,
    ).reshape(answers, steps, 4 * HEAD)

    prefill_out = pl.pallas_call(
        unpack_kernel,
        out_shape=jax.ShapeDtypeStruct((HEAD, UNITS * HEAD), bf16),
        grid=(2,),
        in_specs=[pl.BlockSpec((UNITS // 2, HEAD, HEAD), lambda i: (i, 0, 0))],
        out_specs=pl.BlockSpec((HEAD, 16 * HEAD), lambda i: (0, i)),
        compiler_params=params,
    )(returned)
    return prefill_out, answer_out


def solution(mesh):
    fine = Mesh(mesh.devices.reshape(4, 2, 2, 4, 4), ("x", "core", "z", "y", "prompt"))
    tokens = P(("prompt", "x", "core", "z", "y"), None)
    rows = P(("prompt", "x", "core"), None, ("z", "y"))
    return jax.shard_map(
        on_device,
        mesh=fine,
        in_specs=(tokens, tokens, tokens, rows, rows, rows),
        out_specs=(tokens, rows),
        check_vma=False,
    )
```

```python
import math

import jax
import jax.numpy as jnp
from jax import lax
from jax.experimental import pallas as pl
from jax.experimental.pallas import tpu as pltpu
from jax.sharding import Mesh, PartitionSpec as P


HEAD = 128
score_scale = 168.0 ** (-0.5)
scale2 = score_scale * math.log2(math.e)
masked = -1e30
safe_square = (100.0 / scale2) ** 2
VMEM_LIMIT = 66500000
bf16, f32 = jnp.bfloat16, jnp.float32
rows_rows = (((1,), (1,)), ((), ()))

UNITS = 32
SOME = 4
PART = 8
WIDTH = PART * HEAD
PARTS = UNITS // PART


def half_heads():
    return [
        ((2 * p + core) * 4 + y, 2 * y + p, core)
        for p in range(2)
        for core in range(2)
        for y in range(4)
    ]


def pack_keys_kernel(k_ref, v_ref, out_ref):
    for to, g, core in half_heads():
        at = g * HEAD
        if core == 0:
            out_ref[to] = k_ref[:, at : at + HEAD]
        else:
            out_ref[to] = v_ref[:, at : at + HEAD].T


def pack_queries_kernel(q_ref, out_ref):
    for to, g, core in half_heads():
        at = (2 * g + core) * HEAD
        out_ref[to] = q_ref[:, at : at + HEAD]


def pack_answers_kernel(aq_ref, ak_ref, av_ref, kept_ref, sent_ref, near_ref):
    odd = lax.axis_index("x") % 2
    here = lax.axis_index("core")
    rows = kept_ref.shape[1]
    q_rows = aq_ref[...].reshape(rows, 4 * HEAD)
    k_rows = ak_ref[...].reshape(rows, 2 * HEAD)
    v_rows = av_ref[...].reshape(rows, 2 * HEAD)
    for p in range(2):
        at = (odd + p) % 2
        near_ref[at, :, :HEAD] = k_rows[:, p * HEAD : (p + 1) * HEAD]
        near_ref[at, :, HEAD:] = v_rows[:, p * HEAD : (p + 1) * HEAD]
        both = [q_rows[:, (2 * p + core) * HEAD : (2 * p + core + 1) * HEAD] for core in range(2)]
        kept_ref[at] = jnp.where(here == 0, both[0], both[1])
        sent_ref[at] = jnp.where(here == 0, both[1], both[0])


def unpack_kernel(in_ref, out_ref):
    for place, g, core in half_heads():
        at = (2 * g + core) * HEAD
        out_ref[:, at : at + HEAD] = in_ref[place]


def copies(core, own_ref, got_ref, ks, vt, sems, part):
    at = pl.ds(part * PART, PART)
    key_ref, value_ref = (own_ref, got_ref) if core == 0 else (got_ref, own_ref)
    return (
        pltpu.make_async_copy(key_ref.at[at], ks.at[at], sems.at[0, part]),
        pltpu.make_async_copy(value_ref.at[at], vt.at[at], sems.at[1, part]),
    )


def start_keys(part, *refs):
    here = lax.axis_index("core")
    for core in range(2):

        @pl.when(here == core)
        def _():
            for copy in copies(core, *refs, part):
                copy.start()


def wait_keys(part, *refs):
    for copy in copies(0, *refs, part):
        copy.wait()


def largest_square(rows):
    squares = lax.dot_general(
        jnp.ones((16, HEAD), bf16), rows * rows, rows_rows, preferred_element_type=f32
    )
    return jnp.max(squares)


def add_keys(q, keys, values_t, allowed, first, acc, tot, top, shifted):
    s = lax.dot_general(keys, q, rows_rows, preferred_element_type=f32)
    if allowed is not None:
        few = allowed.shape[1]
        seen = jnp.where(allowed, s[:, :few], masked)
        s = seen if few == s.shape[1] else jnp.concatenate([seen, s[:, few:]], axis=1)
    n, w = s.shape
    s = s * scale2
    if shifted:
        old = top[:, first:]
        new = jnp.maximum(old, jnp.max(s, axis=0, keepdims=True))
        shrink = jnp.exp2(old - new)
        s = s - new
        top[:, first:] = new
        tot[:, first:] = tot[:, first:] * shrink
        acc[:, first:] = acc[:, first:] * shrink
    p = jnp.exp2(s)
    tot[:, first:] += jnp.sum(p.reshape(n // 8, 8, w), axis=0)
    acc[:, first:] += jnp.dot(values_t, p.astype(bf16), preferred_element_type=f32)


def key_block(ks, vt, n, count):
    keys = ks[pl.ds(n, count)].reshape(count * HEAD, HEAD)
    values_t = jnp.concatenate([vt[n + i] for i in range(count)], axis=1)
    return keys, values_t


def either(safe, run):
    @pl.when(safe)
    def _():
        run(False)

    @pl.when(jnp.logical_not(safe))
    def _():
        run(True)


def square_kernel(q_ref, square_ref):
    square_ref[...] = jnp.full_like(square_ref, largest_square(q_ref[...].reshape(-1, HEAD)))


def prompt_kernel(
    q_square, k_square_0, k_square_1, q_ref, own_0, got_0, own_1, got_1, o_ref, ks, vt, acc, tot, top, sems
):
    i = pl.program_id(0)
    z = lax.axis_index("z")
    sides = [
        (own, got, ks.at[h], vt.at[h], sems.at[h])
        for h, (own, got) in enumerate(((own_0, got_0), (own_1, got_1)))
    ]

    @pl.when(i == 0)
    def _():
        for part in range(PARTS):
            for side in sides:
                start_keys(part, *side)

    q = q_ref[...].reshape(WIDTH, HEAD)
    k_square = jnp.maximum(k_square_0[0, 0], k_square_1[0, 0])
    safe = q_square[0, 0] * k_square <= safe_square
    acc[...] = jnp.zeros_like(acc)
    tot[...] = jnp.zeros_like(tot)
    for side in sides:
        wait_keys(i, *side)

    def run(shifted):
        top[...] = jnp.full_like(top, masked if shifted else 0.0)

        def body(t, carry):
            blocks = [key_block(ks.at[h], vt.at[h], t * PART, PART) for h in range(2)]
            keys = jnp.concatenate([k for k, _ in blocks], axis=0)
            values_t = jnp.concatenate([v for _, v in blocks], axis=1)
            add_keys(q, keys, values_t, None, 0, acc, tot, top, shifted)
            return carry

        lax.fori_loop(0, i, body, 0)
        wide = SOME * HEAD
        key = lax.broadcasted_iota(jnp.int32, (2 * wide, wide), 0)
        row = lax.broadcasted_iota(jnp.int32, (1, wide), 1)
        allowed = (key <= row) | (key >= wide)

        def diagonal(skip):
            for c in range(PART // SOME):
                blocks = [key_block(ks.at[0], vt.at[0], i * PART + c * SOME, SOME)]
                if c >= skip:
                    at = i * PART + (c - skip) * SOME
                    blocks.append(key_block(ks.at[1], vt.at[1], at, SOME))
                keys = jnp.concatenate([k for k, _ in blocks], axis=0)
                values_t = jnp.concatenate([v for _, v in blocks], axis=1)
                first = c * wide
                add_keys(
                    q[first:], keys, values_t, allowed[: len(blocks) * wide], first,
                    acc, tot, top, shifted,
                )

        @pl.when(z == 1)
        def _():
            diagonal(0)

        @pl.when(z == 0)
        def _():
            diagonal(1)

    either(safe, run)
    total = jnp.sum(tot[...], axis=0, keepdims=True)
    o_ref[...] = (acc[...] * (1.0 / total)).astype(bf16).T.reshape(PART, HEAD, HEAD)


def answer_queries(refs):
    parts = [ref[:, at : at + HEAD] for ref in refs for at in (0, HEAD)]
    return jnp.concatenate(parts, axis=0)


def answer_near(refs, peer_ref, at):
    parts = []
    for n, ref in enumerate(refs):
        parts.append(ref[:, 2 * HEAD + at : 3 * HEAD + at])
        parts.append(peer_ref[n, :, at : at + HEAD])
    return jnp.concatenate(parts, axis=0)


def own_answer_kernel(
    a0, a1, a2, a3, peer_ref, own_ref, got_ref, acc, tot, top, k_square, ks, vt, sems
):
    side = (own_ref, got_ref, ks, vt, sems)
    for part in range(PARTS):
        start_keys(part, *side)
    here = lax.axis_index("x") // 2 == lax.axis_index("z")
    refs = (a0, a1, a2, a3)
    q = answer_queries(refs)
    near_keys, near_values = (answer_near(refs, peer_ref, at) for at in (0, HEAD))
    count = q.shape[0]
    for part in range(PARTS):
        wait_keys(part, *side)
    most = largest_square(ks[...].reshape(-1, HEAD))
    k_square[...] = jnp.full_like(k_square, most)
    acc[...] = jnp.zeros_like(acc)
    tot[...] = jnp.zeros_like(tot)
    top[...] = jnp.zeros_like(top)

    @pl.when(here)
    def _():
        most_near = jnp.maximum(most, largest_square(near_keys))
        safe = largest_square(q) * most_near <= safe_square

        def run(shifted):
            if shifted:
                top[...] = jnp.full_like(top, masked)
            u = lax.broadcasted_iota(jnp.int32, (count, count), 0)
            t = lax.broadcasted_iota(jnp.int32, (1, count), 1)
            allowed = (u >= t - t % 4) & (u <= t)
            add_keys(q, near_keys, near_values.T, allowed, 0, acc, tot, top, shifted)

            def body(part, carry):
                keys, values_t = key_block(ks, vt, part * PART, PART)
                add_keys(q, keys, values_t, None, 0, acc, tot, top, shifted)
                return carry

            lax.fori_loop(0, PARTS, body, 0)

        either(safe, run)


def other_answer_kernel(
    k_square, a0, a1, a2, a3, own_ref, got_ref, acc_in, tot_in, top_in,
    kept_ref, sent_ref, ks, vt, acc, tot, top, sems,
):
    here = lax.axis_index("x") // 2 == lax.axis_index("z")
    side = (own_ref, got_ref, ks, vt, sems)

    @pl.when(jnp.logical_not(here))
    def _():
        kept_ref[...] = jnp.zeros_like(kept_ref)
        sent_ref[...] = jnp.zeros_like(sent_ref)

    @pl.when(here)
    def _():
        for part in range(PARTS):
            start_keys(part, *side)
        q = answer_queries((a0, a1, a2, a3))
        acc[...] = acc_in[...]
        tot[...] = tot_in[...]
        top[...] = top_in[...]
        safe = (largest_square(q) * k_square[0, 0] <= safe_square) & (
            jnp.max(jnp.abs(top_in[...])) == 0.0
        )

        def run(shifted):
            def body(part, carry):
                wait_keys(part, *side)
                keys, values_t = key_block(ks, vt, part * PART, PART)
                add_keys(q, keys, values_t, None, 0, acc, tot, top, shifted)
                return carry

            lax.fori_loop(0, PARTS, body, 0)

        either(safe, run)
        total = jnp.sum(tot[...], axis=0, keepdims=True)
        out = (acc[...] * (1.0 / total)).astype(bf16).T.reshape(4, 2, -1, HEAD)
        kept_ref[...] = out[:, 0]
        sent_ref[...] = out[:, 1]


def on_device(queries, keys, values, answer_query_rows, answer_key_rows, answer_value_rows):
    params = pltpu.CompilerParams(vmem_limit_bytes=VMEM_LIMIT)
    units = ("x", "core", "y")
    swap = [(0, 1), (1, 0)]
    x, core, z = (lax.axis_index(name) for name in ("x", "core", "z"))
    whole = pl.BlockSpec(memory_space=pltpu.VMEM)
    outside = pl.BlockSpec(memory_space=pltpu.HBM)
    scalars = pl.BlockSpec(memory_space=pltpu.SMEM)
    unit_shape = jax.ShapeDtypeStruct((UNITS, HEAD, HEAD), bf16)
    answers, steps = answer_query_rows.shape[:2]
    rows = answers * steps

    def move(array, axis, by):
        return lax.ppermute(array, axis, [(r, (r + by) % 4) for r in range(4)])

    packed_keys = pl.pallas_call(
        pack_keys_kernel,
        out_shape=unit_shape,
        grid=(2,),
        in_specs=[pl.BlockSpec((HEAD, 8 * HEAD), lambda i: (0, i))] * 2,
        out_specs=pl.BlockSpec((UNITS // 2, HEAD, HEAD), lambda i: (i, 0, 0)),
        compiler_params=params,
    )(keys, values)
    near_shape = jax.ShapeDtypeStruct((2, rows, HEAD), bf16)
    kept, sent, near = pl.pallas_call(
        pack_answers_kernel,
        out_shape=(near_shape, near_shape, jax.ShapeDtypeStruct((2, rows, 2 * HEAD), bf16)),
        in_specs=[whole] * 3,
        out_specs=(whole,) * 3,
        compiler_params=params,
        cost_estimate=pl.CostEstimate(flops=0, bytes_accessed=1 << 18, transcendentals=0),
    )(answer_query_rows, answer_key_rows, answer_value_rows)
    packed_queries = pl.pallas_call(
        pack_queries_kernel,
        out_shape=unit_shape,
        grid=(2,),
        in_specs=[pl.BlockSpec((HEAD, 16 * HEAD), lambda i: (0, i))],
        out_specs=pl.BlockSpec((UNITS // 2, HEAD, HEAD), lambda i: (i, 0, 0)),
        compiler_params=params,
        cost_estimate=pl.CostEstimate(flops=0, bytes_accessed=2 << 20, transcendentals=0),
    )(queries)

    mixed = jnp.concatenate([kept, lax.ppermute(sent, "core", swap), near], axis=-1)
    same, opposite = mixed[0], mixed[1]
    asked = (same, move(opposite, "x", 1), move(same, "x", 2), move(opposite, "x", 3))

    own_0 = lax.all_to_all(packed_keys, units, split_axis=0, concat_axis=0, tiled=True)
    own_0, packed_queries, *asked = lax.optimization_barrier((own_0, packed_queries, *asked))
    near = jnp.stack([rows_of[:, 2 * HEAD :] for rows_of in asked])
    peer = lax.ppermute(near, "core", swap)
    own_1 = lax.ppermute(own_0, "z", swap)
    got_0 = lax.ppermute(own_0, "core", swap)
    head_queries = lax.all_to_all(packed_queries, units, split_axis=0, concat_axis=0, tiled=True)

    key_scratch = [pltpu.VMEM((UNITS, HEAD, HEAD), bf16)] * 2
    key_sems = [pltpu.SemaphoreType.DMA((2, PARTS))]
    state_sizes = (HEAD, 8, 1)
    *state, k_square = pl.pallas_call(
        own_answer_kernel,
        out_shape=tuple(jax.ShapeDtypeStruct((n, 8 * rows), f32) for n in state_sizes)
        + (jax.ShapeDtypeStruct((8, HEAD), f32),),
        in_specs=[whole] * 5 + [outside] * 2,
        out_specs=(whole,) * 4,
        scratch_shapes=key_scratch + key_sems,
        compiler_params=params,
        cost_estimate=pl.CostEstimate(flops=5 << 30, bytes_accessed=2 << 20, transcendentals=1 << 21),
    )(*asked, peer, own_0, got_0)
    k_square_1 = lax.ppermute(k_square, "z", swap)
    own_1, k_square_1, head_queries = lax.optimization_barrier((own_1, k_square_1, head_queries))
    got_1 = lax.ppermute(own_1, "core", swap)

    q_square = pl.pallas_call(
        square_kernel,
        out_shape=jax.ShapeDtypeStruct((8, HEAD), f32),
        in_specs=[whole],
        out_specs=whole,
        compiler_params=params,
        cost_estimate=pl.CostEstimate(flops=1 << 30, bytes_accessed=1 << 20, transcendentals=0),
    )(head_queries)
    pairs = UNITS * HEAD * 2 * UNITS * HEAD // 2
    attended = pl.pallas_call(
        prompt_kernel,
        out_shape=unit_shape,
        grid=(PARTS,),
        in_specs=[scalars] * 3 + [pl.BlockSpec((PART, HEAD, HEAD), lambda i: (i, 0, 0))]
        + [outside] * 4,
        out_specs=pl.BlockSpec((PART, HEAD, HEAD), lambda i: (i, 0, 0)),
        scratch_shapes=[pltpu.VMEM((2, UNITS, HEAD, HEAD), bf16)] * 2
        + [pltpu.VMEM((n, WIDTH), f32) for n in state_sizes]
        + [pltpu.SemaphoreType.DMA((2, 2, PARTS))],
        compiler_params=params,
        cost_estimate=pl.CostEstimate(
            flops=8 * HEAD * pairs, bytes_accessed=6 << 20, transcendentals=pairs
        ),
    )(q_square, k_square, k_square_1, head_queries, own_0, got_0, own_1, got_1)
    returned = lax.all_to_all(attended, units, split_axis=0, concat_axis=0, tiled=True)

    state = lax.optimization_barrier((attended, *state))[1:]
    answer_shape = jax.ShapeDtypeStruct((4, rows, HEAD), bf16)
    kept, sent = pl.pallas_call(
        other_answer_kernel,
        out_shape=(answer_shape, answer_shape),
        in_specs=[scalars] + [whole] * 4 + [outside] * 2 + [whole] * 3,
        out_specs=(whole, whole),
        scratch_shapes=key_scratch
        + [pltpu.VMEM((n, 8 * rows), f32) for n in state_sizes]
        + key_sems,
        compiler_params=params,
        cost_estimate=pl.CostEstimate(flops=5 << 30, bytes_accessed=2 << 20, transcendentals=1 << 21),
    )(k_square_1, *asked, own_1, got_1, *state)
    back = lax.ppermute(sent, "core", swap)
    pair = jnp.concatenate(
        [jnp.where(core == 0, kept, back), jnp.where(core == 0, back, kept)], axis=-1
    )
    four = jnp.stack([pair[0]] + [move(pair[by], "x", -by) for by in (1, 2, 3)])
    answer_out = jnp.concatenate(
        [lax.dynamic_index_in_dim(four, (2 * z + p - x) % 4, 0, False) for p in range(2)],
        axis=-1,
    ).reshape(answers, steps, 4 * HEAD)

    prefill_out = pl.pallas_call(
        unpack_kernel,
        out_shape=jax.ShapeDtypeStruct((HEAD, UNITS * HEAD), bf16),
        grid=(2,),
        in_specs=[pl.BlockSpec((UNITS // 2, HEAD, HEAD), lambda i: (i, 0, 0))],
        out_specs=pl.BlockSpec((HEAD, 16 * HEAD), lambda i: (0, i)),
        compiler_params=params,
    )(returned)
    return prefill_out, answer_out


def solution(mesh):
    fine = Mesh(mesh.devices.reshape(4, 2, 2, 4, 4), ("x", "core", "z", "y", "prompt"))
    tokens = P(("prompt", "x", "core", "z", "y"), None)
    rows = P(("prompt", "x", "core"), None, ("z", "y"))
    return jax.shard_map(
        on_device,
        mesh=fine,
        in_specs=(tokens, tokens, tokens, rows, rows, rows),
        out_specs=(tokens, rows),
        check_vma=False,
    )
```

```python
import math

import jax
import jax.numpy as jnp
from jax import lax
from jax.experimental import pallas as pl
from jax.experimental.pallas import tpu as pltpu
from jax.sharding import Mesh, PartitionSpec as P


HEAD = 128
score_scale = 168.0 ** (-0.5)
scale2 = score_scale * math.log2(math.e)
masked = -1e30
safe_square = (100.0 / scale2) ** 2
VMEM_LIMIT = 66500000
bf16, f32 = jnp.bfloat16, jnp.float32
rows_rows = (((1,), (1,)), ((), ()))

UNITS = 32
SOME = 4
PART = 8
WIDTH = PART * HEAD
PARTS = UNITS // PART


def half_heads():
    return [
        ((2 * p + core) * 4 + y, 2 * y + p, core)
        for p in range(2)
        for core in range(2)
        for y in range(4)
    ]


def pack_keys_kernel(k_ref, v_ref, out_ref):
    for to, g, core in half_heads():
        at = g * HEAD
        if core == 0:
            out_ref[to] = k_ref[:, at : at + HEAD]
        else:
            out_ref[to] = v_ref[:, at : at + HEAD].T


def pack_queries_kernel(q_ref, out_ref):
    for to, g, core in half_heads():
        at = (2 * g + core) * HEAD
        out_ref[to] = q_ref[:, at : at + HEAD]


def pack_answers_kernel(aq_ref, ak_ref, av_ref, kept_ref, sent_ref, near_ref):
    odd = lax.axis_index("x") % 2
    here = lax.axis_index("core")
    rows = kept_ref.shape[1]
    q_rows = aq_ref[...].reshape(rows, 4 * HEAD)
    k_rows = ak_ref[...].reshape(rows, 2 * HEAD)
    v_rows = av_ref[...].reshape(rows, 2 * HEAD)
    for p in range(2):
        at = (odd + p) % 2
        near_ref[at, :, :HEAD] = k_rows[:, p * HEAD : (p + 1) * HEAD]
        near_ref[at, :, HEAD:] = v_rows[:, p * HEAD : (p + 1) * HEAD]
        both = [q_rows[:, (2 * p + core) * HEAD : (2 * p + core + 1) * HEAD] for core in range(2)]
        kept_ref[at] = jnp.where(here == 0, both[0], both[1])
        sent_ref[at] = jnp.where(here == 0, both[1], both[0])


def unpack_kernel(in_ref, out_ref):
    for place, g, core in half_heads():
        at = (2 * g + core) * HEAD
        out_ref[:, at : at + HEAD] = in_ref[place]


def copies(core, own_ref, got_ref, ks, vt, sems, part):
    at = pl.ds(part * PART, PART)
    key_ref, value_ref = (own_ref, got_ref) if core == 0 else (got_ref, own_ref)
    return (
        pltpu.make_async_copy(key_ref.at[at], ks.at[at], sems.at[0, part]),
        pltpu.make_async_copy(value_ref.at[at], vt.at[at], sems.at[1, part]),
    )


def start_keys(part, *refs):
    here = lax.axis_index("core")
    for core in range(2):

        @pl.when(here == core)
        def _():
            for copy in copies(core, *refs, part):
                copy.start()


def wait_keys(part, *refs):
    for copy in copies(0, *refs, part):
        copy.wait()


def largest_square(rows):
    squares = lax.dot_general(
        jnp.ones((16, HEAD), bf16), rows * rows, rows_rows, preferred_element_type=f32
    )
    return jnp.max(squares)


def add_keys(q, keys, values_t, allowed, first, acc, tot, top, shifted):
    s = lax.dot_general(keys, q, rows_rows, preferred_element_type=f32)
    if allowed is not None:
        few = allowed.shape[1]
        seen = jnp.where(allowed, s[:, :few], masked)
        s = seen if few == s.shape[1] else jnp.concatenate([seen, s[:, few:]], axis=1)
    n, w = s.shape
    s = s * scale2
    if shifted:
        old = top[:, first:]
        new = jnp.maximum(old, jnp.max(s, axis=0, keepdims=True))
        shrink = jnp.exp2(old - new)
        s = s - new
        top[:, first:] = new
        tot[:, first:] = tot[:, first:] * shrink
        acc[:, first:] = acc[:, first:] * shrink
    p = jnp.exp2(s)
    tot[:, first:] += jnp.sum(p.reshape(n // 8, 8, w), axis=0)
    acc[:, first:] += jnp.dot(values_t, p.astype(bf16), preferred_element_type=f32)


def key_block(ks, vt, n, count):
    keys = ks[pl.ds(n, count)].reshape(count * HEAD, HEAD)
    values_t = jnp.concatenate([vt[n + i] for i in range(count)], axis=1)
    return keys, values_t


def either(safe, run):
    @pl.when(safe)
    def _():
        run(False)

    @pl.when(jnp.logical_not(safe))
    def _():
        run(True)


def square_kernel(q_ref, square_ref):
    square_ref[...] = jnp.full_like(square_ref, largest_square(q_ref[...].reshape(-1, HEAD)))


def prompt_kernel(
    q_square, k_square_0, k_square_1, q_ref, own_0, got_0, own_1, got_1, o_ref, ks, vt, acc, tot, top, sems
):
    i = pl.program_id(0)
    z = lax.axis_index("z")
    sides = [
        (own, got, ks.at[h], vt.at[h], sems.at[h])
        for h, (own, got) in enumerate(((own_0, got_0), (own_1, got_1)))
    ]

    @pl.when(i == 0)
    def _():
        for part in range(PARTS):
            for side in sides:
                start_keys(part, *side)

    q = q_ref[...].reshape(WIDTH, HEAD)
    k_square = jnp.maximum(k_square_0[0, 0], k_square_1[0, 0])
    safe = q_square[0, 0] * k_square <= safe_square
    acc[...] = jnp.zeros_like(acc)
    tot[...] = jnp.zeros_like(tot)
    for side in sides:
        wait_keys(i, *side)

    def run(shifted):
        top[...] = jnp.full_like(top, masked if shifted else 0.0)

        def body(t, carry):
            blocks = [key_block(ks.at[h], vt.at[h], t * PART, PART) for h in range(2)]
            keys = jnp.concatenate([k for k, _ in blocks], axis=0)
            values_t = jnp.concatenate([v for _, v in blocks], axis=1)
            add_keys(q, keys, values_t, None, 0, acc, tot, top, shifted)
            return carry

        lax.fori_loop(0, i, body, 0)
        wide = SOME * HEAD
        key = lax.broadcasted_iota(jnp.int32, (2 * wide, wide), 0)
        row = lax.broadcasted_iota(jnp.int32, (1, wide), 1)
        allowed = (key <= row) | (key >= wide)

        def diagonal(skip):
            for c in range(PART // SOME):
                blocks = [key_block(ks.at[0], vt.at[0], i * PART + c * SOME, SOME)]
                if c >= skip:
                    at = i * PART + (c - skip) * SOME
                    blocks.append(key_block(ks.at[1], vt.at[1], at, SOME))
                keys = jnp.concatenate([k for k, _ in blocks], axis=0)
                values_t = jnp.concatenate([v for _, v in blocks], axis=1)
                first = c * wide
                add_keys(
                    q[first:], keys, values_t, allowed[: len(blocks) * wide], first,
                    acc, tot, top, shifted,
                )

        @pl.when(z == 1)
        def _():
            diagonal(0)

        @pl.when(z == 0)
        def _():
            diagonal(1)

    either(safe, run)
    total = jnp.sum(tot[...], axis=0, keepdims=True)
    o_ref[...] = (acc[...] * (1.0 / total)).astype(bf16).T.reshape(PART, HEAD, HEAD)


def answer_queries(refs):
    parts = [ref[:, at : at + HEAD] for ref in refs for at in (0, HEAD)]
    return jnp.concatenate(parts, axis=0)


def answer_near(refs, peer_ref, at):
    parts = []
    for n, ref in enumerate(refs):
        parts.append(ref[:, 2 * HEAD + at : 3 * HEAD + at])
        parts.append(peer_ref[n, :, at : at + HEAD])
    return jnp.concatenate(parts, axis=0)


def own_answer_kernel(
    a0, a1, a2, a3, peer_ref, own_ref, got_ref, acc, tot, top, k_square, ks, vt, sems
):
    side = (own_ref, got_ref, ks, vt, sems)
    for part in range(PARTS):
        start_keys(part, *side)
    here = lax.axis_index("x") // 2 == lax.axis_index("z")
    refs = (a0, a1, a2, a3)
    q = answer_queries(refs)
    near_keys, near_values = (answer_near(refs, peer_ref, at) for at in (0, HEAD))
    count = q.shape[0]
    for part in range(PARTS):
        wait_keys(part, *side)
    most = largest_square(ks[...].reshape(-1, HEAD))
    k_square[...] = jnp.full_like(k_square, most)
    acc[...] = jnp.zeros_like(acc)
    tot[...] = jnp.zeros_like(tot)
    top[...] = jnp.zeros_like(top)

    @pl.when(here)
    def _():
        most_near = jnp.maximum(most, largest_square(near_keys))
        safe = largest_square(q) * most_near <= safe_square

        def run(shifted):
            if shifted:
                top[...] = jnp.full_like(top, masked)
            u = lax.broadcasted_iota(jnp.int32, (count, count), 0)
            t = lax.broadcasted_iota(jnp.int32, (1, count), 1)
            allowed = (u >= t - t % 4) & (u <= t)
            add_keys(q, near_keys, near_values.T, allowed, 0, acc, tot, top, shifted)

            def body(part, carry):
                keys, values_t = key_block(ks, vt, part * PART, PART)
                add_keys(q, keys, values_t, None, 0, acc, tot, top, shifted)
                return carry

            lax.fori_loop(0, PARTS, body, 0)

        either(safe, run)


def other_answer_kernel(
    k_square, a0, a1, a2, a3, own_ref, got_ref, acc_in, tot_in, top_in,
    kept_ref, sent_ref, ks, vt, acc, tot, top, sems,
):
    here = lax.axis_index("x") // 2 == lax.axis_index("z")
    side = (own_ref, got_ref, ks, vt, sems)

    @pl.when(jnp.logical_not(here))
    def _():
        kept_ref[...] = jnp.zeros_like(kept_ref)
        sent_ref[...] = jnp.zeros_like(sent_ref)

    @pl.when(here)
    def _():
        for part in range(PARTS):
            start_keys(part, *side)
        q = answer_queries((a0, a1, a2, a3))
        acc[...] = acc_in[...]
        tot[...] = tot_in[...]
        top[...] = top_in[...]
        safe = (largest_square(q) * k_square[0, 0] <= safe_square) & (
            jnp.max(jnp.abs(top_in[...])) == 0.0
        )

        def run(shifted):
            def body(part, carry):
                wait_keys(part, *side)
                keys, values_t = key_block(ks, vt, part * PART, PART)
                add_keys(q, keys, values_t, None, 0, acc, tot, top, shifted)
                return carry

            lax.fori_loop(0, PARTS, body, 0)

        either(safe, run)
        total = jnp.sum(tot[...], axis=0, keepdims=True)
        out = (acc[...] * (1.0 / total)).astype(bf16).T.reshape(4, 2, -1, HEAD)
        kept_ref[...] = out[:, 0]
        sent_ref[...] = out[:, 1]


def on_device(queries, keys, values, answer_query_rows, answer_key_rows, answer_value_rows):
    params = pltpu.CompilerParams(vmem_limit_bytes=VMEM_LIMIT)
    units = ("x", "core", "y")
    swap = [(0, 1), (1, 0)]
    x, core, z = (lax.axis_index(name) for name in ("x", "core", "z"))
    whole = pl.BlockSpec(memory_space=pltpu.VMEM)
    outside = pl.BlockSpec(memory_space=pltpu.HBM)
    scalars = pl.BlockSpec(memory_space=pltpu.SMEM)
    unit_shape = jax.ShapeDtypeStruct((UNITS, HEAD, HEAD), bf16)
    answers, steps = answer_query_rows.shape[:2]
    rows = answers * steps

    def move(array, axis, by):
        return lax.ppermute(array, axis, [(r, (r + by) % 4) for r in range(4)])

    packed_keys = pl.pallas_call(
        pack_keys_kernel,
        out_shape=unit_shape,
        grid=(2,),
        in_specs=[pl.BlockSpec((HEAD, 8 * HEAD), lambda i: (0, i))] * 2,
        out_specs=pl.BlockSpec((UNITS // 2, HEAD, HEAD), lambda i: (i, 0, 0)),
        compiler_params=params,
    )(keys, values)
    near_shape = jax.ShapeDtypeStruct((2, rows, HEAD), bf16)
    kept, sent, near = pl.pallas_call(
        pack_answers_kernel,
        out_shape=(near_shape, near_shape, jax.ShapeDtypeStruct((2, rows, 2 * HEAD), bf16)),
        in_specs=[whole] * 3,
        out_specs=(whole,) * 3,
        compiler_params=params,
        cost_estimate=pl.CostEstimate(flops=0, bytes_accessed=1 << 18, transcendentals=0),
    )(answer_query_rows, answer_key_rows, answer_value_rows)
    packed_queries = pl.pallas_call(
        pack_queries_kernel,
        out_shape=unit_shape,
        grid=(2,),
        in_specs=[pl.BlockSpec((HEAD, 16 * HEAD), lambda i: (0, i))],
        out_specs=pl.BlockSpec((UNITS // 2, HEAD, HEAD), lambda i: (i, 0, 0)),
        compiler_params=params,
        cost_estimate=pl.CostEstimate(flops=0, bytes_accessed=2 << 20, transcendentals=0),
    )(queries)

    mixed = jnp.concatenate([kept, lax.ppermute(sent, "core", swap), near], axis=-1)
    same, opposite = mixed[0], mixed[1]
    pairs = [(2 * ((r + 2) % 4) + side, 2 * r + side) for side in range(2) for r in (2 * side, 2 * side + 1)]
    far = lax.ppermute(same, ("x", "z"), pairs)
    asked = (same, move(opposite, "x", 1), far, move(opposite, "x", 3))

    own_0 = lax.all_to_all(packed_keys, units, split_axis=0, concat_axis=0, tiled=True)
    own_0, packed_queries, *asked = lax.optimization_barrier((own_0, packed_queries, *asked))
    near = jnp.stack([rows_of[:, 2 * HEAD :] for rows_of in asked])
    peer = lax.ppermute(near, "core", swap)
    own_1 = lax.ppermute(own_0, "z", swap)
    got_0 = lax.ppermute(own_0, "core", swap)
    head_queries = lax.all_to_all(packed_queries, units, split_axis=0, concat_axis=0, tiled=True)

    key_scratch = [pltpu.VMEM((UNITS, HEAD, HEAD), bf16)] * 2
    key_sems = [pltpu.SemaphoreType.DMA((2, PARTS))]
    state_sizes = (HEAD, 8, 1)
    *state, k_square = pl.pallas_call(
        own_answer_kernel,
        out_shape=tuple(jax.ShapeDtypeStruct((n, 8 * rows), f32) for n in state_sizes)
        + (jax.ShapeDtypeStruct((8, HEAD), f32),),
        in_specs=[whole] * 5 + [outside] * 2,
        out_specs=(whole,) * 4,
        scratch_shapes=key_scratch + key_sems,
        compiler_params=params,
        cost_estimate=pl.CostEstimate(flops=5 << 30, bytes_accessed=2 << 20, transcendentals=1 << 21),
    )(*asked, peer, own_0, got_0)
    k_square_1 = lax.ppermute(k_square, "z", swap)
    own_1, k_square_1, head_queries = lax.optimization_barrier((own_1, k_square_1, head_queries))
    got_1 = lax.ppermute(own_1, "core", swap)

    q_square = pl.pallas_call(
        square_kernel,
        out_shape=jax.ShapeDtypeStruct((8, HEAD), f32),
        in_specs=[whole],
        out_specs=whole,
        compiler_params=params,
        cost_estimate=pl.CostEstimate(flops=1 << 30, bytes_accessed=1 << 20, transcendentals=0),
    )(head_queries)
    pairs = UNITS * HEAD * 2 * UNITS * HEAD // 2
    attended = pl.pallas_call(
        prompt_kernel,
        out_shape=unit_shape,
        grid=(PARTS,),
        in_specs=[scalars] * 3 + [pl.BlockSpec((PART, HEAD, HEAD), lambda i: (i, 0, 0))]
        + [outside] * 4,
        out_specs=pl.BlockSpec((PART, HEAD, HEAD), lambda i: (i, 0, 0)),
        scratch_shapes=[pltpu.VMEM((2, UNITS, HEAD, HEAD), bf16)] * 2
        + [pltpu.VMEM((n, WIDTH), f32) for n in state_sizes]
        + [pltpu.SemaphoreType.DMA((2, 2, PARTS))],
        compiler_params=params,
        cost_estimate=pl.CostEstimate(
            flops=8 * HEAD * pairs, bytes_accessed=6 << 20, transcendentals=pairs
        ),
    )(q_square, k_square, k_square_1, head_queries, own_0, got_0, own_1, got_1)
    returned = lax.all_to_all(attended, units, split_axis=0, concat_axis=0, tiled=True)

    state = lax.optimization_barrier((attended, *state))[1:]
    answer_shape = jax.ShapeDtypeStruct((4, rows, HEAD), bf16)
    kept, sent = pl.pallas_call(
        other_answer_kernel,
        out_shape=(answer_shape, answer_shape),
        in_specs=[scalars] + [whole] * 4 + [outside] * 2 + [whole] * 3,
        out_specs=(whole, whole),
        scratch_shapes=key_scratch
        + [pltpu.VMEM((n, 8 * rows), f32) for n in state_sizes]
        + key_sems,
        compiler_params=params,
        cost_estimate=pl.CostEstimate(flops=5 << 30, bytes_accessed=2 << 20, transcendentals=1 << 21),
    )(k_square_1, *asked, own_1, got_1, *state)
    back = lax.ppermute(sent, "core", swap)
    pair = jnp.concatenate(
        [jnp.where(core == 0, kept, back), jnp.where(core == 0, back, kept)], axis=-1
    )
    four = jnp.stack([pair[0]] + [move(pair[by], "x", -by) for by in (1, 2, 3)])
    answer_out = jnp.concatenate(
        [lax.dynamic_index_in_dim(four, (2 * z + p - x) % 4, 0, False) for p in range(2)],
        axis=-1,
    ).reshape(answers, steps, 4 * HEAD)

    prefill_out = pl.pallas_call(
        unpack_kernel,
        out_shape=jax.ShapeDtypeStruct((HEAD, UNITS * HEAD), bf16),
        grid=(2,),
        in_specs=[pl.BlockSpec((UNITS // 2, HEAD, HEAD), lambda i: (i, 0, 0))],
        out_specs=pl.BlockSpec((HEAD, 16 * HEAD), lambda i: (0, i)),
        compiler_params=params,
    )(returned)
    return prefill_out, answer_out


def solution(mesh):
    fine = Mesh(mesh.devices.reshape(4, 2, 2, 4, 4), ("x", "core", "z", "y", "prompt"))
    tokens = P(("prompt", "x", "core", "z", "y"), None)
    rows = P(("prompt", "x", "core"), None, ("z", "y"))
    return jax.shard_map(
        on_device,
        mesh=fine,
        in_specs=(tokens, tokens, tokens, rows, rows, rows),
        out_specs=(tokens, rows),
        check_vma=False,
    )
```
